32 devices in a mesh: clips: 2 (over y), tm: 4 (over z), space: 4 (over x, core).
Axes of the slice: x: 2, y: 2, z: 4, core: 2. Of those that a mesh axis runs over, the one named last changes fastest.
Arguments:
- latent: bfloat16 [16, 8, 16, 16], P(('clips', 'tm'), 'space'), parts along dimension 0, may hold values from -6 to 6
- w_in: bfloat16 [3, 3, 3, 16, 384], replicated, may hold values from -0.3125 to 0.3125
- b_in: float32 [384], replicated, may hold values from -1.5 to 1.5
- gain_in: float32 [384], replicated, may hold values from 0.1 to 1.9
- w_time: bfloat16 [3, 384, 768], replicated, may hold values from -0.1875 to 0.1875
- b_time: float32 [768], replicated, may hold values from -1.5 to 1.5
- w_up: bfloat16 [3, 3, 384, 192], replicated, may hold values from -0.109375 to 0.109375
- b_up: float32 [192], replicated, may hold values from -1.5 to 1.5
Outputs:
- decoded: bfloat16 [32, 16, 32, 192], P(('clips', 'tm'), 'space'), parts along dimension 0
The draws below stay inside these ranges and needn't reach their ends.
There are 2 independent parts, one for each index of `clips`. The reference program is written for one: setup_inputs(seed, part) draws one part's arguments, and reference() takes and returns one part's arrays. A program takes and returns all parts, laid end to end along the dimension named above; an argument that names none is the same for every part. Nothing has to cross between parts.
All inputs are finite; a program needn't handle non-finite values.
Results may differ from the reference program's by a relative error of at most 0.0055.
Values may be sent and summed in bfloat16 or wider, within the bound.
No kernel may reach another device: no remote copies, remote signals or barrier semaphores. Data moves between devices by JAX's collectives and lax.ppermute only.
A program may use at most 64 MiB of HBM per device.

```python
import jax
import jax.numpy as jnp
from jax import lax

ZC = 16
CH = 384
CO = 192
W = 16
FRAMES = 8
ROWS = 8


def levels(rng, extent, shards, low, high):
    gain, own = 1.0, jax.random.fold_in(rng, 6)
    for position, parts in shards:
        steps = jnp.exp(jax.random.uniform(jax.random.fold_in(own, position), (parts,), jnp.float32, low / len(shards), high / len(shards)))
        gain = gain * jnp.repeat(steps, extent[position] // parts).reshape([-1 if axis == position else 1 for axis in range(len(extent))])
    return gain


def bell_draw(own_key, shape, spread, limit, cuts=(), kind=jnp.bfloat16):
    loudness = levels(own_key, shape, cuts, -0.22, 0.18) if cuts else 1.0
    entries = jax.random.normal(own_key, shape, jnp.float32) * spread * loudness
    return jnp.minimum(jnp.maximum(entries, -limit), limit).astype(kind)


def setup_inputs(seed: int = 0, part: int = 0) -> dict:
    seeds = jax.random.split(jax.random.key(seed), 9)
    part_splits = jax.random.split(jax.random.fold_in(seeds[8], part), 9)
    return {
        "latent": bell_draw(part_splits[0], (FRAMES, ROWS, W, ZC), 1.0, 6.0, ((0, 4), (1, 4))),
        "w_in": bell_draw(seeds[1], (3, 3, 3, ZC, CH), (27 * ZC) ** -0.5, 0.3125),
        "b_in": bell_draw(seeds[2], (CH,), 0.3, 1.5, (), jnp.float32),
        "gain_in": jnp.clip(1.0 + 0.18 * jax.random.normal(seeds[3], (CH,), jnp.float32), 0.1, 1.9),
        "w_time": bell_draw(seeds[4], (3, CH, 2 * CH), (3 * CH) ** -0.5, 0.1875),
        "b_time": bell_draw(seeds[5], (2 * CH,), 0.3, 1.5, (), jnp.float32),
        "w_up": bell_draw(seeds[6], (3, 3, CH, CO), (9 * CH) ** -0.5, 0.109375),
        "b_up": bell_draw(seeds[7], (CO,), 0.3, 1.5, (), jnp.float32),
    }


EPSILON = 1e-06

def normalize_silu(hidden, gain_in):
    inverse = lax.rsqrt(lax.optimization_barrier(jnp.mean(hidden * hidden, axis=1, keepdims=True)) + EPSILON)
    return jax.nn.silu(hidden * inverse * gain_in).astype(jnp.bfloat16)

def plane_conv(padded_frame, w_up, b_up):
    row_count = padded_frame.shape[0] - 2
    col_count = padded_frame.shape[1] - 2
    tap_list = [padded_frame[row_tap:row_tap + row_count, col_tap:col_tap + col_count, :] for row_tap in range(3) for col_tap in range(3)]
    stacked = jnp.concatenate(tap_list, axis=2).reshape(row_count * col_count, -1)
    result = jnp.dot(stacked, w_up.reshape(stacked.shape[1], -1), preferred_element_type=jnp.float32) + b_up
    return result.astype(jnp.bfloat16).reshape(row_count, col_count, -1)

def reference(latent, w_in, b_in, gain_in, w_time, b_time, w_up, b_up):
    frame_count, row_count, col_count, latent_width = latent.shape
    padded = jnp.pad(latent, ((2, 0), (1, 1), (1, 1), (0, 0)))
    tap_list = [padded[frame_tap:frame_tap + frame_count, row_tap:row_tap + row_count, col_tap:col_tap + col_count, :] for frame_tap in range(3) for row_tap in range(3) for col_tap in range(3)]
    stacked = jnp.concatenate(tap_list, axis=3).reshape(frame_count * row_count * col_count, 27 * latent_width)
    hidden = jnp.dot(stacked, w_in.reshape(27 * latent_width, -1), preferred_element_type=jnp.float32) + b_in
    active = normalize_silu(hidden, gain_in).reshape(frame_count, row_count, col_count, -1)
    feature_width = active.shape[3]
    delayed = jnp.pad(active, ((2, 0), (0, 0), (0, 0), (0, 0)))
    tap_list = [delayed[frame_tap:frame_tap + frame_count] for frame_tap in range(3)]
    stacked = jnp.concatenate(tap_list, axis=3).reshape(frame_count * row_count * col_count, 3 * feature_width)
    timed = (jnp.dot(stacked, w_time.reshape(3 * feature_width, -1), preferred_element_type=jnp.float32) + b_time).astype(jnp.bfloat16)
    timed = timed.reshape(frame_count, row_count, col_count, 2, feature_width)
    doubled = jnp.moveaxis(timed, 3, 1).reshape(2 * frame_count, row_count, col_count, feature_width)
    enlarged = jnp.repeat(jnp.repeat(doubled, 2, axis=1), 2, axis=2)
    padded_up = jnp.pad(enlarged, ((0, 0), (1, 1), (1, 1), (0, 0)))

    def one_frame(padded_frame):
        return plane_conv(padded_frame, w_up, b_up)
    return lax.map(one_frame, padded_up)
```

```python
import functools

import jax
import jax.numpy as jnp
from jax import lax
from jax.experimental import pallas as pl
from jax.experimental.pallas import tpu as pltpu
from jax.sharding import PartitionSpec as P

EPSILON = 1e-06
LANES = 128


def swapped(x, axis, first):
    count = lax.axis_size(axis)
    pairs = []
    for low in range(first, first + count, 2):
        a, b = low % count, (low + 1) % count
        pairs += [(a, b), (b, a)]
    return lax.ppermute(x, axis, pairs)


def shifted(x, axis, by):
    count = lax.axis_size(axis)
    return lax.ppermute(x, axis, [(i, (i + by) % count) for i in range(count)])


def pack_kernel(own_ref, even_ref, odd_ref, packed_ref):
    space, count = lax.axis_index("space"), lax.axis_size("space")
    frames, rows, cols, width = own_ref.shape
    is_even = lax.rem(space, 2) == 0
    even, odd = even_ref[...], odd_ref[...]
    above = jnp.where(space > 0, jnp.where(is_even, odd, even), jnp.zeros_like(even))
    below = jnp.where(space < count - 1, jnp.where(is_even, even, odd), jnp.zeros_like(even))
    channel = lax.broadcasted_iota(jnp.int32, (width, LANES), 0)
    lane = lax.broadcasted_iota(jnp.int32, (width, LANES), 1)
    total = jnp.zeros((frames * cols, LANES), jnp.float32)
    for r, block in enumerate([x[:, r] for x in (above, own_ref[...], below) for r in range(rows)]):
        spread = (lane == channel + r * width).astype(own_ref.dtype)
        total += jnp.dot(block.reshape(frames * cols, width), spread, preferred_element_type=jnp.float32)
    packed_ref[...] = total.astype(own_ref.dtype).reshape(packed_ref.shape)


def stage_kernel(*refs):
    count = (len(refs) - 1) // 2
    copies = [pltpu.make_async_copy(refs[i], refs[count + i], refs[-1].at[i]) for i in range(count)]
    for copy in copies:
        copy.start()
    for copy in copies:
        copy.wait()


def column_shift(x, by, cols):
    column = lax.rem(lax.broadcasted_iota(jnp.int32, x.shape, 0), cols)
    edge = 0 if by > 0 else cols - 1
    return jnp.where(column == edge, 0.0, pltpu.roll(x, by % x.shape[0], axis=0))


def main_kernel(
    own_ref, one_ref, two_ref, w_in_ref, b_in_ref, gain_ref, w_time_ref, b_time_ref, w_up_ref, b_up_ref, out_ref,
    *, rows, width,
):
    time, space, space_count = lax.axis_index("tm"), lax.axis_index("space"), lax.axis_size("space")
    own_frames, cols, _ = own_ref.shape
    tall = rows + 2
    features = w_in_ref.shape[1]
    one = jnp.where(time > 0, one_ref[...], jnp.zeros_like(one_ref))
    two = jnp.where(time > 1, two_ref[...], jnp.zeros_like(two_ref))
    frames = jnp.concatenate([two, one, own_ref[...]], axis=0).astype(jnp.float32)
    frame_total = frames.shape[0]
    flat = frames.reshape(frame_total * cols, LANES)
    taps = []
    for shift in (1, 0, -1):
        moved = column_shift(flat, shift, cols) if shift else flat
        rolled = [moved if r == 0 else pltpu.roll(moved, LANES - r * width, axis=1) for r in range(tall)]
        stacked = jnp.stack([x.astype(jnp.bfloat16).reshape(frame_total, cols, LANES) for x in rolled], axis=1)
        taps.append(stacked.reshape(frame_total * tall * cols, LANES))
    block = tall * cols
    active_frames = frame_total - 2
    left, right = [], []
    blank = jnp.zeros((LANES - 3 * width, features), jnp.bfloat16)
    for a in range(3):
        for e in range(3):
            left.append(taps[e][a * block : (a + active_frames) * block])
            for b in range(3):
                start = ((a * 3 + b) * 3 + e) * width
                right.append(w_in_ref[start : start + width, :])
            right.append(blank)
    hidden = jnp.dot(
        jnp.concatenate(left, axis=1), jnp.concatenate(right, axis=0), preferred_element_type=jnp.float32
    )
    hidden = hidden + b_in_ref[...][None, :]
    inverse = lax.rsqrt(jnp.mean(hidden * hidden, axis=1, keepdims=True) + EPSILON)
    v = hidden * inverse * gain_ref[...][None, :]
    half = 0.5 * v
    active = half + half * jnp.tanh(half)
    frame_id = lax.broadcasted_iota(jnp.int32, active.shape, 0) // block
    active = jnp.where((frame_id >= active_frames - own_frames) | (time > 0), active, 0.0).astype(jnp.bfloat16)

    stacked = jnp.concatenate([active[a * block : (a + own_frames) * block] for a in range(3)], axis=1)
    timed = jnp.dot(stacked, w_time_ref[...], preferred_element_type=jnp.float32) + b_time_ref[...][None, :]
    row = lax.rem(lax.broadcasted_iota(jnp.int32, timed.shape, 0) // cols, tall)
    inside = ((row > 0) | (space > 0)) & ((row < tall - 1) | (space < space_count - 1))
    timed = jnp.where(inside, timed, 0.0).astype(jnp.bfloat16)

    out_rows = 2 * rows
    out_width = w_up_ref.shape[0] // 9
    left = []
    for b in range(3):
        picks = []
        for f in range(own_frames):
            for h in range(2):
                for i in range(out_rows):
                    r = (i + b - 1) // 2 + 1
                    picks.append(timed[(f * tall + r) * cols : (f * tall + r + 1) * cols, h * features : (h + 1) * features])
        left.append(jnp.concatenate(picks, axis=0))
    sums = []
    for e in range(3):
        total = None
        for b in range(3):
            tap = w_up_ref[(b * 3 + e) * out_width : (b * 3 + e + 1) * out_width, :]
            part = lax.dot_general(left[b], tap, (((1,), (1,)), ((), ())), preferred_element_type=jnp.float32)
            total = part if total is None else total + part
        sums.append(total)
    middle = sums[1] + b_up_ref[...][None, :]
    even = column_shift(sums[0], 1, cols) + (middle + sums[2])
    odd = column_shift(sums[2], -1, cols) + (middle + sums[0])
    both = jnp.stack([even, odd], axis=1).reshape(2 * even.shape[0], out_width)
    out_ref[...] = both.astype(jnp.bfloat16).reshape(out_ref.shape)


def shards(latent, w_in, b_in, gain_in, w_time, b_time, w_up, b_up):
    own_frames, rows, cols, width = latent.shape
    features = w_in.shape[-1]
    out_width = w_up.shape[-1]
    vmem = pl.BlockSpec(memory_space=pltpu.VMEM)
    even = swapped(latent, "space", 0)
    odd = swapped(latent, "space", 1)
    own = pl.pallas_call(
        pack_kernel,
        out_shape=jax.ShapeDtypeStruct((own_frames, cols, LANES), latent.dtype),
        in_specs=[vmem] * 3,
        out_specs=vmem,
        compiler_params=pltpu.CompilerParams(vmem_limit_bytes=1024 * 1024),
    )(latent, even, odd)
    two = shifted(own, "tm", 2)
    one = shifted(own, "tm", 1)
    weights = (
        w_in.reshape(-1, features), b_in, gain_in, w_time.reshape(-1, w_time.shape[-1]), b_time,
        jnp.swapaxes(w_up, 2, 3).reshape(-1, w_up.shape[2]), b_up,
    )
    staged = pl.pallas_call(
        stage_kernel,
        out_shape=[pltpu.VMEM(w.shape, w.dtype) for w in weights],
        in_specs=[pl.BlockSpec(memory_space=pltpu.HBM)] * len(weights),
        out_specs=[vmem] * len(weights),
        scratch_shapes=[pltpu.SemaphoreType.DMA((len(weights),))],
        compiler_params=pltpu.CompilerParams(vmem_limit_bytes=1024 * 1024),
    )(*[pltpu.with_memory_space_constraint(w, pltpu.HBM) for w in weights])
    return pl.pallas_call(
        functools.partial(main_kernel, rows=rows, width=width),
        out_shape=jax.ShapeDtypeStruct((2 * own_frames, 2 * rows, 2 * cols, out_width), jnp.bfloat16),
        in_specs=[vmem] * 10,
        out_specs=vmem,
        compiler_params=pltpu.CompilerParams(vmem_limit_bytes=16 * 1024 * 1024),
    )(own, one, two, *staged)


def solution(mesh):
    in_specs = (P(("clips", "tm"), "space", None, None), P(), P(), P(), P(), P(), P(), P())
    out_specs = P(("clips", "tm"), "space", None, None)
    return jax.shard_map(shards, mesh=mesh, in_specs=in_specs, out_specs=out_specs, check_vma=False)
```

```python
import functools

import jax
import jax.numpy as jnp
from jax import lax
from jax.experimental import pallas as pl
from jax.experimental.pallas import tpu as pltpu
from jax.sharding import PartitionSpec as P

EPSILON = 1e-06
LANES = 128
VMEM = pl.BlockSpec(memory_space=pltpu.VMEM)
HBM = pl.BlockSpec(memory_space=pltpu.HBM)


def swapped(x, axis, first):
    count = lax.axis_size(axis)
    pairs = []
    for low in range(first, first + count, 2):
        a, b = low % count, (low + 1) % count
        pairs += [(a, b), (b, a)]
    return lax.ppermute(x, axis, pairs)


def shifted(x, axis, by):
    count = lax.axis_size(axis)
    return lax.ppermute(x, axis, [(i, (i + by) % count) for i in range(count)])


def in_hbm(x):
    return pltpu.with_memory_space_constraint(x, pltpu.HBM)


def copies_of(sources, targets, sems):
    return [pltpu.make_async_copy(s, t, sems.at[i]) for i, (s, t) in enumerate(zip(sources, targets))]


def stage_kernel(*refs):
    count = len(refs) // 2
    copies = copies_of(refs[:count], refs[count:-1], refs[-1])
    first = lax.axis_index("tm") == 0

    @pl.when(first)
    def _():
        for copy in copies[-2:]:
            copy.start()

    for copy in copies[:-2]:
        copy.start()
    for copy in copies[:-2]:
        copy.wait()

    @pl.when(first)
    def _():
        for copy in copies[-2:]:
            copy.wait()


def pack_kernel(odd_ref, even_ref, own_ref, packed_ref):
    space, count = lax.axis_index("space"), lax.axis_size("space")
    frames, rows, cols, width = own_ref.shape
    is_even = lax.rem(space, 2) == 0
    even, odd = even_ref[...], odd_ref[...]
    above = jnp.where(space > 0, jnp.where(is_even, odd, even), jnp.zeros_like(even))
    below = jnp.where(space < count - 1, jnp.where(is_even, even, odd), jnp.zeros_like(even))
    channel = lax.broadcasted_iota(jnp.int32, (width, LANES), 0)
    lane = lax.broadcasted_iota(jnp.int32, (width, LANES), 1)
    total = jnp.zeros((frames * cols, LANES), jnp.float32)
    for r, block in enumerate([x[:, r] for x in (above, own_ref[...], below) for r in range(rows)]):
        spread = (lane == channel + r * width).astype(own_ref.dtype)
        total += jnp.dot(block.reshape(frames * cols, width), spread, preferred_element_type=jnp.float32)
    packed_ref[...] = total.astype(own_ref.dtype).reshape(packed_ref.shape)


def column_shift(x, by, cols):
    groups = x.shape[0] // cols
    column = lax.broadcasted_iota(jnp.int32, (groups, cols, x.shape[1]), 1).reshape(x.shape)
    edge = 0 if by > 0 else cols - 1
    return jnp.where(column == edge, 0.0, pltpu.roll(x, by % x.shape[0], axis=0))


def entry(frames, w_in_ref, b_in_ref, gain_ref, rows, width):
    frame_total, cols, _ = frames.shape
    features = w_in_ref.shape[1]
    tall = rows + 2
    block = tall * cols
    reach = 3 * width
    flat = frames.astype(jnp.float32).reshape(frame_total * cols, LANES)
    lane = lax.broadcasted_iota(jnp.int32, flat.shape, 1)
    west, east = column_shift(flat, 1, cols), column_shift(flat, -1, cols)

    def window(x, r, at):
        return pltpu.roll(x, (at - r * width) % LANES, axis=1) if at != r * width else x

    def by_position(parts):
        parts = [x.astype(jnp.bfloat16).reshape(frame_total, cols, LANES) for x in parts]
        return jnp.stack(parts, axis=1).reshape(frame_total * block, LANES)

    pair = by_position([jnp.where(lane < reach, window(west, r, 0), window(flat, r, reach)) for r in range(tall)])
    later = jnp.concatenate([east[cols:], east[:cols]], axis=0)
    last = by_position([jnp.where(lane < reach, window(east, r, 0), window(later, r, reach)) for r in range(tall)])
    size = (frame_total - 2) * block
    left = [pair[a * block : a * block + size] for a in range(3)] + [last[:size], last[2 * block : 2 * block + size]]

    def taps(a, e):
        return [w_in_ref[((a * 3 + b) * 3 + e) * width : ((a * 3 + b) * 3 + e + 1) * width, :] for b in range(3)]

    gap = [jnp.zeros((LANES - 2 * reach, features), jnp.bfloat16)]
    right = []
    for a in range(3):
        right += taps(a, 0) + taps(a, 1) + gap
    right += taps(0, 2) + taps(1, 2) + gap
    right += taps(2, 2) + [jnp.zeros((LANES - reach, features), jnp.bfloat16)]
    hidden = jnp.dot(
        jnp.concatenate(left, axis=1), jnp.concatenate(right, axis=0), preferred_element_type=jnp.float32
    )
    hidden = hidden + b_in_ref[...][None, :]
    inverse = lax.rsqrt(jnp.mean(hidden * hidden, axis=1, keepdims=True) + EPSILON)
    half = hidden * inverse * (0.5 * gain_ref[...][None, :])
    return (half + half * jnp.tanh(half)).astype(jnp.bfloat16)


def own_part(active, w_time_ref):
    features = active.shape[1]
    block = active.shape[0] // 2
    early, late = active[:block], active[block:]
    left = jnp.concatenate(
        [jnp.concatenate([jnp.zeros_like(early), early], axis=1), jnp.concatenate([early, late], axis=1)], axis=0
    )
    return jnp.dot(left, w_time_ref[features:, :], preferred_element_type=jnp.float32)


def earlier_part(active, w_time_ref):
    features = active.shape[1]
    block = active.shape[0] // 2
    early, late = active[:block], active[block:]
    left = jnp.concatenate(
        [jnp.concatenate([early, late], axis=1), jnp.concatenate([late, jnp.zeros_like(late)], axis=1)], axis=0
    )
    return jnp.dot(left, w_time_ref[: 2 * features, :], preferred_element_type=jnp.float32)


def add_row_taps(w_up_ref, w_sum_ref):
    size = w_sum_ref.shape[0] // 2
    top, middle, bottom = (w_up_ref[b * size : (b + 1) * size, :].astype(jnp.float32) for b in range(3))
    w_sum_ref[:size, :] = (middle + bottom).astype(w_sum_ref.dtype)
    w_sum_ref[size:, :] = (top + middle).astype(w_sum_ref.dtype)


def upsample(timed, w_up_ref, w_sum_ref, b_up_ref, wide_ref, done_ref, rows, cols):
    space, space_count = lax.axis_index("space"), lax.axis_size("space")
    features = timed.shape[1] // 2
    tall = rows + 2
    frames = timed.shape[0] // (tall * cols)
    out_width = done_ref.shape[-1]
    timed = timed.astype(jnp.bfloat16)

    def timed_row(f, h, r):
        x = timed[(f * tall + r) * cols : (f * tall + r + 1) * cols, h * features : (h + 1) * features]
        if r == 0:
            x = jnp.where(space > 0, x, jnp.zeros_like(x))
        if r == tall - 1:
            x = jnp.where(space < space_count - 1, x, jnp.zeros_like(x))
        return x

    doubled = [[timed_row(f, h, r) for r in range(tall)] for f in range(frames) for h in range(2)]
    tap_size = 3 * out_width
    for p in range(2):
        left = jnp.concatenate(
            [jnp.concatenate([frame[r + p + k] for frame in doubled for r in range(rows)], axis=0) for k in range(2)], axis=1
        )
        sums = []
        for e in range(3):
            outer = w_up_ref[(2 * p * 3 + e) * out_width : (2 * p * 3 + e + 1) * out_width, :]
            inner = w_sum_ref[p * tap_size + e * out_width : p * tap_size + (e + 1) * out_width, :]
            tap = jnp.concatenate([inner, outer] if p else [outer, inner], axis=1)
            sums.append(lax.dot_general(left, tap, (((1,), (1,)), ((), ())), preferred_element_type=jnp.float32))
        middle = sums[1] + b_up_ref[...][None, :]
        even = column_shift(sums[0], 1, cols) + (middle + sums[2])
        odd = column_shift(sums[2], -1, cols) + (middle + sums[0])
        for q, x in enumerate((even, odd)):
            low = x[:, :LANES]
            high = jnp.concatenate([x[:, LANES:]] * (LANES // (out_width - LANES)), axis=1)
            for i in range(2 * frames * rows):
                at = (i // rows) * 2 * rows + 2 * (i % rows) + p
                wide_ref[0, at, pl.ds(q, cols, stride=2), :] = low[i * cols : (i + 1) * cols]
                wide_ref[1, at, pl.ds(q, cols, stride=2), :] = high[i * cols : (i + 1) * cols]
    whole = jnp.concatenate([wide_ref[0], wide_ref[1][:, :, : out_width - LANES]], axis=2)
    done_ref[...] = whole.astype(done_ref.dtype).reshape(done_ref.shape)


def send_out(done_ref, out_ref, sem):
    copy = pltpu.make_async_copy(done_ref, out_ref, sem)
    copy.start()
    copy.wait()


def first_kernel(
    own_ref, w_in_ref, b_in_ref, gain_ref, b_time_ref, b_up_ref, w_time_hbm, w_up_hbm, _w_time, _w_up,
    out_ref, w_time_ref, w_up_ref, w_sum_ref, wide_ref, done_ref, sems, *, rows, width,
):
    first = lax.axis_index("tm") == 0
    cols = own_ref.shape[1]

    @pl.when(first)
    def _():
        add_row_taps(w_up_ref, w_sum_ref)
        own = own_ref[...]
        active = entry(jnp.concatenate([jnp.zeros_like(own), own], axis=0), w_in_ref, b_in_ref, gain_ref, rows, width)
        timed = own_part(active, w_time_ref) + b_time_ref[...][None, :]
        upsample(timed, w_up_ref, w_sum_ref, b_up_ref, wide_ref, done_ref, rows, cols)
        send_out(done_ref, out_ref, sems.at[2])

    @pl.when(jnp.logical_not(first))
    def _():
        time_copy, up_copy = copies_of((w_time_hbm, w_up_hbm), (w_time_ref, w_up_ref), sems)
        up_copy.start()
        time_copy.start()
        up_copy.wait()
        add_row_taps(w_up_ref, w_sum_ref)
        time_copy.wait()


def own_kernel(own_ref, one_ref, w_in_ref, b_in_ref, gain_ref, b_time_ref, w_time_ref, timed_ref, *, rows, width):
    @pl.when(lax.axis_index("tm") > 0)
    def _():
        active = entry(jnp.concatenate([one_ref[...], own_ref[...]], axis=0), w_in_ref, b_in_ref, gain_ref, rows, width)
        timed_ref[...] = own_part(active, w_time_ref) + b_time_ref[...][None, :]


def last_kernel(
    one_ref, two_ref, timed_ref, w_in_ref, b_in_ref, gain_ref, b_up_ref, w_time_ref, w_up_ref, w_sum_ref, _out,
    out_ref, wide_ref, done_ref, sem, *, rows, width,
):
    time = lax.axis_index("tm")

    @pl.when(time > 0)
    def _():
        two = jnp.where(time > 1, two_ref[...], jnp.zeros_like(two_ref))
        active = entry(jnp.concatenate([two, one_ref[...]], axis=0), w_in_ref, b_in_ref, gain_ref, rows, width)
        timed = timed_ref[...] + earlier_part(active, w_time_ref)
        upsample(timed, w_up_ref, w_sum_ref, b_up_ref, wide_ref, done_ref, rows, one_ref.shape[1])
        send_out(done_ref, out_ref, sem)


def params(mib):
    return pltpu.CompilerParams(vmem_limit_bytes=mib * 1024 * 1024)


def shards(latent, w_in, b_in, gain_in, w_time, b_time, w_up, b_up):
    frames, rows, cols, width = latent.shape
    features = w_in.shape[-1]
    out_width = w_up.shape[-1]
    w_time = in_hbm(w_time.reshape(-1, w_time.shape[-1]))
    w_up = in_hbm(jnp.swapaxes(w_up, 2, 3).reshape(-1, w_up.shape[2]))
    large = [pltpu.VMEM(w.shape, w.dtype) for w in (w_time, w_up)]
    out_shape = (2 * frames, 2 * rows, 2 * cols, out_width)
    sizes = dict(rows=rows, width=width)

    even = swapped(latent, "space", 0)
    odd = swapped(latent, "space", 1)
    arrays = [in_hbm(x) for x in (w_in.reshape(-1, features), b_in, gain_in, b_time, b_up, latent)] + [w_time, w_up]
    w_in, b_in, gain_in, b_time, b_up, own, w_time_kept, w_up_kept = pl.pallas_call(
        stage_kernel,
        out_shape=[pltpu.VMEM(x.shape, x.dtype) for x in arrays],
        in_specs=[HBM] * len(arrays),
        out_specs=[VMEM] * len(arrays),
        scratch_shapes=[pltpu.SemaphoreType.DMA((len(arrays),))],
        compiler_params=params(1),
    )(*arrays)
    own = pl.pallas_call(
        pack_kernel,
        out_shape=pltpu.VMEM((frames, cols, LANES), latent.dtype),
        in_specs=[VMEM] * 3,
        out_specs=VMEM,
        compiler_params=params(1),
    )(odd, even, own)
    one = shifted(own, "tm", 1)
    two = shifted(own, "tm", 2)

    finish = [
        pltpu.VMEM((2, 2 * frames * 2 * rows, 2 * cols, LANES), jnp.float32),
        pltpu.VMEM(out_shape, jnp.bfloat16),
    ]
    out, w_time_kept, w_up_kept, w_sum = pl.pallas_call(
        functools.partial(first_kernel, **sizes),
        out_shape=[pltpu.HBM(out_shape, jnp.bfloat16)] + large + [pltpu.VMEM((6 * out_width, features), jnp.bfloat16)],
        in_specs=[VMEM] * 6 + [HBM] * 2 + [VMEM] * 2,
        out_specs=[HBM] + [VMEM] * 3,
        scratch_shapes=finish + [pltpu.SemaphoreType.DMA((3,))],
        input_output_aliases={8: 1, 9: 2},
        compiler_params=params(16),
    )(own, w_in, b_in, gain_in, b_time, b_up, w_time, w_up, w_time_kept, w_up_kept)
    timed = pl.pallas_call(
        functools.partial(own_kernel, **sizes),
        out_shape=pltpu.VMEM((frames * (rows + 2) * cols, 2 * features), jnp.float32),
        in_specs=[VMEM] * 7,
        out_specs=VMEM,
        compiler_params=params(16),
    )(own, one, w_in, b_in, gain_in, b_time, w_time_kept)
    return pl.pallas_call(
        functools.partial(last_kernel, **sizes),
        out_shape=pltpu.HBM(out_shape, jnp.bfloat16),
        in_specs=[VMEM] * 10 + [HBM],
        out_specs=HBM,
        scratch_shapes=finish + [pltpu.SemaphoreType.DMA],
        input_output_aliases={10: 0},
        compiler_params=params(16),
    )(one, two, timed, w_in, b_in, gain_in, b_up, w_time_kept, w_up_kept, w_sum, out)


def solution(mesh):
    in_specs = (P(("clips", "tm"), "space", None, None), P(), P(), P(), P(), P(), P(), P())
    out_specs = P(("clips", "tm"), "space", None, None)
    return jax.shard_map(shards, mesh=mesh, in_specs=in_specs, out_specs=out_specs, check_vma=False)
```

```python
import functools

import jax
import jax.numpy as jnp
from jax import lax
from jax.experimental import pallas as pl
from jax.experimental.pallas import tpu as pltpu
from jax.sharding import PartitionSpec as P

EPSILON = 1e-06
LANES = 128
VMEM = pl.BlockSpec(memory_space=pltpu.VMEM)
HBM = pl.BlockSpec(memory_space=pltpu.HBM)


def swapped(x, axis, first):
    count = lax.axis_size(axis)
    pairs = []
    for low in range(first, first + count, 2):
        a, b = low % count, (low + 1) % count
        pairs += [(a, b), (b, a)]
    return lax.ppermute(x, axis, pairs)


def shifted(x, axis, by):
    count = lax.axis_size(axis)
    return lax.ppermute(x, axis, [(i, (i + by) % count) for i in range(count)])


def in_hbm(x):
    return pltpu.with_memory_space_constraint(x, pltpu.HBM)


def copies_of(sources, targets, sems):
    return [pltpu.make_async_copy(s, t, sems.at[i]) for i, (s, t) in enumerate(zip(sources, targets))]


def stage_kernel(*refs):
    count = len(refs) // 2
    copies = copies_of(refs[:count], refs[count:-1], refs[-1])
    early = lax.axis_index("tm") <= 1

    @pl.when(early)
    def _():
        for copy in copies[-2:]:
            copy.start()

    for copy in copies[:-2]:
        copy.start()
    for copy in copies[:-2]:
        copy.wait()

    @pl.when(early)
    def _():
        for copy in copies[-2:]:
            copy.wait()


def pack_kernel(odd_ref, even_ref, own_ref, w_up_ref, packed_ref, taps_ref):
    time = lax.axis_index("tm")
    space, count = lax.axis_index("space"), lax.axis_size("space")
    frames, rows, cols, width = own_ref.shape
    is_even = lax.rem(space, 2) == 0
    even, odd = even_ref[...], odd_ref[...]
    above = jnp.where(space > 0, jnp.where(is_even, odd, even), jnp.zeros_like(even))
    below = jnp.where(space < count - 1, jnp.where(is_even, even, odd), jnp.zeros_like(even))
    channel = lax.broadcasted_iota(jnp.int32, (width, LANES), 0)
    lane = lax.broadcasted_iota(jnp.int32, (width, LANES), 1)
    total = jnp.zeros((frames * cols, LANES), jnp.float32)
    for r, block in enumerate([x[:, r] for x in (above, own_ref[...], below) for r in range(rows)]):
        spread = (lane == channel + r * width).astype(own_ref.dtype)
        total += jnp.dot(block.reshape(frames * cols, width), spread, preferred_element_type=jnp.float32)
    packed_ref[...] = total.astype(own_ref.dtype).reshape(packed_ref.shape)

    @pl.when(time == 0)
    def _():
        prepare_taps(w_up_ref, taps_ref)


def column_shift(x, by, cols):
    groups = x.shape[0] // cols
    column = lax.broadcasted_iota(jnp.int32, (groups, cols, x.shape[1]), 1).reshape(x.shape)
    edge = 0 if by > 0 else cols - 1
    return jnp.where(column == edge, 0.0, pltpu.roll(x, by % x.shape[0], axis=0))


def column_taps(frames, rows, width):
    frame_total, cols, _ = frames.shape
    tall = rows + 2
    reach = 3 * width
    flat = frames.astype(jnp.float32).reshape(frame_total * cols, LANES)
    lane = lax.broadcasted_iota(jnp.int32, flat.shape, 1)
    west, east = column_shift(flat, 1, cols), column_shift(flat, -1, cols)
    later = jnp.concatenate([east[cols:], east[:cols]], axis=0)

    def window(x, r, at):
        return pltpu.roll(x, (at - r * width) % LANES, axis=1) if at != r * width else x

    def by_position(x, y):
        parts = [jnp.where(lane < reach, window(x, r, 0), window(y, r, reach)) for r in range(tall)]
        parts = [part.astype(jnp.bfloat16).reshape(frame_total, cols, LANES) for part in parts]
        return jnp.stack(parts, axis=1).reshape(frame_total * tall * cols, LANES)

    return by_position(west, flat), by_position(east, later)


def weight_taps(w_in_ref, width, taps):
    rows = [
        w_in_ref[((a * 3 + b) * 3 + e) * width : ((a * 3 + b) * 3 + e + 1) * width, :] for a, e in taps for b in range(3)
    ]
    return rows + [jnp.zeros((LANES - len(rows) * width, w_in_ref.shape[1]), jnp.bfloat16)]


def entry(frames, w_in_ref, b_in_ref, rows, width):
    pair, last = column_taps(frames, rows, width)
    block = (rows + 2) * frames.shape[1]
    size = (frames.shape[0] - 2) * block
    left = [pair[a * block : a * block + size] for a in range(3)] + [last[:size], last[2 * block : 2 * block + size]]
    right = []
    for taps in [[(a, 0), (a, 1)] for a in range(3)] + [[(0, 2), (1, 2)], [(2, 2)]]:
        right += weight_taps(w_in_ref, width, taps)
    left, right = jnp.concatenate(left, axis=1), jnp.concatenate(right, axis=0)
    return jnp.dot(left, right, preferred_element_type=jnp.float32) + b_in_ref[...][None, :]


def entry_of_two(frames, w_in_ref, rows, width):
    pair, last = column_taps(jnp.concatenate([frames, jnp.zeros_like(frames[:1])], axis=0), rows, width)
    block = (rows + 2) * frames.shape[1]
    left = [pair[: 2 * block], pair[block:], last[: 2 * block]]
    right = []
    for taps in ([(0, 0), (0, 1)], [(1, 0), (1, 1)], [(0, 2), (1, 2)]):
        right += weight_taps(w_in_ref, width, taps)
    left, right = jnp.concatenate(left, axis=1), jnp.concatenate(right, axis=0)
    return jnp.dot(left, right, preferred_element_type=jnp.float32)


def normalized(hidden, gain_ref):
    inverse = lax.rsqrt(jnp.mean(hidden * hidden, axis=1, keepdims=True) + EPSILON)
    half = hidden * inverse * (0.5 * gain_ref[...][None, :])
    return (half + half * jnp.tanh(half)).astype(jnp.bfloat16)


def own_part(active, w_time_ref):
    features = active.shape[1]
    block = active.shape[0] // 2
    early, late = active[:block], active[block:]
    left = jnp.concatenate(
        [jnp.concatenate([jnp.zeros_like(early), early], axis=1), jnp.concatenate([early, late], axis=1)], axis=0
    )
    return jnp.dot(left, w_time_ref[features:, :], preferred_element_type=jnp.float32)


def earlier_part(active, w_time_ref):
    features = active.shape[1]
    block = active.shape[0] // 2
    early, late = active[:block], active[block:]
    left = jnp.concatenate(
        [jnp.concatenate([early, late], axis=1), jnp.concatenate([late, jnp.zeros_like(late)], axis=1)], axis=0
    )
    return jnp.dot(left, w_time_ref[: 2 * features, :], preferred_element_type=jnp.float32)


def prepare_taps(w_up_ref, taps_ref):
    features = w_up_ref.shape[1]
    out_width = taps_ref.shape[-1]
    for e in range(3):
        taps = [w_up_ref[(b * 3 + e) * out_width : (b * 3 + e + 1) * out_width, :].T for b in range(3)]
        top, middle, bottom = (x.astype(jnp.float32) for x in taps)
        taps_ref[0, e, :features] = taps[0]
        taps_ref[0, e, features:] = (middle + bottom).astype(taps_ref.dtype)
        taps_ref[1, e, :features] = (top + middle).astype(taps_ref.dtype)
        taps_ref[1, e, features:] = taps[2]


def upsample(timed, taps_ref, b_up_ref, out_ref, wide_ref, done_ref, sems, rows, cols):
    space, space_count = lax.axis_index("space"), lax.axis_size("space")
    features = timed.shape[1] // 2
    tall = rows + 2
    frames = timed.shape[0] // (tall * cols)
    out_width = done_ref.shape[-1]
    timed = timed.astype(jnp.bfloat16)

    def timed_row(f, h, r):
        x = timed[(f * tall + r) * cols : (f * tall + r + 1) * cols, h * features : (h + 1) * features]
        if r == 0:
            x = jnp.where(space > 0, x, jnp.zeros_like(x))
        if r == tall - 1:
            x = jnp.where(space < space_count - 1, x, jnp.zeros_like(x))
        return x

    doubled = [[timed_row(f, h, r) for r in range(tall)] for f in range(frames) for h in range(2)]
    copies = []
    for p in range(2):
        left = jnp.concatenate(
            [jnp.concatenate([frame[r + p + k] for frame in doubled for r in range(rows)], axis=0) for k in range(2)], axis=1
        )
        sums = [jnp.dot(left, taps_ref[p, e], preferred_element_type=jnp.float32) for e in range(3)]
        middle = sums[1] + b_up_ref[...][None, :]
        even = column_shift(sums[0], 1, cols) + (middle + sums[2])
        odd = column_shift(sums[2], -1, cols) + (middle + sums[0])
        half = even.shape[0]
        for q, x in enumerate((even, odd)):
            wide_ref[p, 0, pl.ds(q, half, stride=2), :] = x[:, :LANES]
            wide_ref[p, 1, pl.ds(q, half, stride=2), pl.ds(0, out_width - LANES)] = x[:, LANES:]
        low, high = wide_ref[p, 0], wide_ref[p, 1, :, pl.ds(0, out_width - LANES)]
        place = done_ref.shape[1:-1]
        done_ref[p, :, :, :, :LANES] = low.astype(done_ref.dtype).reshape(place + (LANES,))
        done_ref[p, :, :, :, LANES:] = high.astype(done_ref.dtype).reshape(place + (out_width - LANES,))
        copies.append(pltpu.make_async_copy(done_ref.at[p], out_ref.at[:, :, p], sems.at[p]))
        copies[-1].start()
    for copy in copies:
        copy.wait()


def first_kernel(
    own_ref, w_in_ref, b_in_ref, gain_ref, b_time_ref, b_up_ref, w_time_hbm, w_up_hbm, _w_time, _w_up, _taps,
    out_ref, w_time_ref, w_up_ref, taps_ref, wide_ref, done_ref, sems, *, rows, width,
):
    time = lax.axis_index("tm")

    @pl.when(time == 0)
    def _():
        own = own_ref[...]
        hidden = entry(jnp.concatenate([jnp.zeros_like(own), own], axis=0), w_in_ref, b_in_ref, rows, width)
        timed = own_part(normalized(hidden, gain_ref), w_time_ref) + b_time_ref[...][None, :]
        upsample(timed, taps_ref, b_up_ref, out_ref, wide_ref, done_ref, sems, rows, own.shape[1])

    @pl.when(time > 1)
    def _():
        time_copy, up_copy = copies_of((w_time_hbm, w_up_hbm), (w_time_ref, w_up_ref), sems)
        up_copy.start()
        time_copy.start()
        up_copy.wait()
        prepare_taps(w_up_ref, taps_ref)
        time_copy.wait()

    @pl.when(time == 1)
    def _():
        prepare_taps(w_up_ref, taps_ref)


def middle_kernel(
    own_ref, one_ref, w_in_ref, b_in_ref, gain_ref, b_time_ref, b_up_ref, w_time_ref, taps_ref, _out,
    out_ref, hidden_ref, timed_ref, wide_ref, done_ref, sems, *, rows, width,
):
    time = lax.axis_index("tm")
    size = hidden_ref.shape[0]

    def known():
        frames = jnp.concatenate([jnp.zeros_like(one_ref), one_ref[...], own_ref[...]], axis=0)
        return entry(frames, w_in_ref, b_in_ref, rows, width)

    @pl.when(time == 1)
    def _():
        active = normalized(known(), gain_ref)
        timed = own_part(active[size:], w_time_ref) + earlier_part(active[:size], w_time_ref) + b_time_ref[...][None, :]
        upsample(timed, taps_ref, b_up_ref, out_ref, wide_ref, done_ref, sems, rows, own_ref.shape[1])

    @pl.when(time > 1)
    def _():
        hidden = known()
        hidden_ref[...] = hidden[:size]
        timed_ref[...] = own_part(normalized(hidden[size:], gain_ref), w_time_ref) + b_time_ref[...][None, :]


def last_kernel(
    two_ref, hidden_ref, timed_ref, w_in_ref, gain_ref, b_up_ref, w_time_ref, taps_ref, _out,
    out_ref, wide_ref, done_ref, sems, *, rows, width,
):
    @pl.when(lax.axis_index("tm") > 1)
    def _():
        active = normalized(hidden_ref[...] + entry_of_two(two_ref[...], w_in_ref, rows, width), gain_ref)
        timed = timed_ref[...] + earlier_part(active, w_time_ref)
        upsample(timed, taps_ref, b_up_ref, out_ref, wide_ref, done_ref, sems, rows, two_ref.shape[1])


def params(mib):
    return pltpu.CompilerParams(vmem_limit_bytes=mib * 1024 * 1024)


def shards(latent, w_in, b_in, gain_in, w_time, b_time, w_up, b_up):
    frames, rows, cols, width = latent.shape
    features = w_in.shape[-1]
    out_width = w_up.shape[-1]
    w_time = in_hbm(w_time.reshape(-1, w_time.shape[-1]))
    w_up = in_hbm(jnp.swapaxes(w_up, 2, 3).reshape(-1, w_up.shape[2]))
    out_shape = (2 * frames, rows, 2, 2 * cols, out_width)

    even = swapped(latent, "space", 0)
    odd = swapped(latent, "space", 1)
    arrays = [in_hbm(x) for x in (w_in.reshape(-1, features), b_in, gain_in, b_time, b_up, latent)] + [w_time, w_up]
    w_in, b_in, gain_in, b_time, b_up, own, w_time_kept, w_up_kept = pl.pallas_call(
        stage_kernel,
        out_shape=[pltpu.VMEM(x.shape, x.dtype) for x in arrays],
        in_specs=[HBM] * len(arrays),
        out_specs=[VMEM] * len(arrays),
        scratch_shapes=[pltpu.SemaphoreType.DMA((len(arrays),))],
        compiler_params=params(1),
    )(*arrays)
    positions = frames * (rows + 2) * cols
    timed_shape = pltpu.VMEM((positions, 2 * features), jnp.float32)
    taps_shape = pltpu.VMEM((2, 3, 2 * features, out_width), jnp.bfloat16)
    own, taps = pl.pallas_call(
        pack_kernel,
        out_shape=[pltpu.VMEM((frames, cols, LANES), latent.dtype), taps_shape],
        in_specs=[VMEM] * 4,
        out_specs=[VMEM] * 2,
        compiler_params=params(4),
    )(odd, even, own, w_up_kept)
    one = shifted(own, "tm", 1)
    two = shifted(own, "tm", 2)

    finish = [
        pltpu.VMEM((2, 2, 2 * frames * rows * 2 * cols, LANES), jnp.float32),
        pltpu.VMEM((2, 2 * frames, rows, 2 * cols, out_width), jnp.bfloat16),
        pltpu.SemaphoreType.DMA((2,)),
    ]
    result = pltpu.HBM(out_shape, jnp.bfloat16)
    out, w_time_kept, w_up_kept, taps = pl.pallas_call(
        functools.partial(first_kernel, rows=rows, width=width),
        out_shape=[result] + [pltpu.VMEM(w.shape, w.dtype) for w in (w_time, w_up)] + [taps_shape],
        in_specs=[VMEM] * 6 + [HBM] * 2 + [VMEM] * 3,
        out_specs=[HBM] + [VMEM] * 3,
        scratch_shapes=finish,
        input_output_aliases={8: 1, 9: 2, 10: 3},
        compiler_params=params(16),
    )(own, w_in, b_in, gain_in, b_time, b_up, w_time, w_up, w_time_kept, w_up_kept, taps)
    out, hidden, timed = pl.pallas_call(
        functools.partial(middle_kernel, rows=rows, width=width),
        out_shape=[result, pltpu.VMEM((positions, features), jnp.float32), timed_shape],
        in_specs=[VMEM] * 9 + [HBM],
        out_specs=[HBM, VMEM, VMEM],
        scratch_shapes=finish,
        input_output_aliases={9: 0},
        compiler_params=params(16),
    )(own, one, w_in, b_in, gain_in, b_time, b_up, w_time_kept, taps, out)
    out = pl.pallas_call(
        functools.partial(last_kernel, rows=rows, width=width),
        out_shape=pltpu.HBM(out_shape, jnp.bfloat16),
        in_specs=[VMEM] * 8 + [HBM],
        out_specs=HBM,
        scratch_shapes=finish,
        input_output_aliases={8: 0},
        compiler_params=params(16),
    )(two, hidden, timed, w_in, gain_in, b_up, w_time_kept, taps, out)
    return out.reshape(2 * frames, 2 * rows, 2 * cols, out_width)


def solution(mesh):
    in_specs = (P(("clips", "tm"), "space", None, None), P(), P(), P(), P(), P(), P(), P())
    out_specs = P(("clips", "tm"), "space", None, None)
    return jax.shard_map(shards, mesh=mesh, in_specs=in_specs, out_specs=out_specs, check_vma=False)
```

```python
import functools

import jax
import jax.numpy as jnp
from jax import lax
from jax.experimental import pallas as pl
from jax.experimental.pallas import tpu as pltpu
from jax.sharding import PartitionSpec as P

EPSILON = 1e-06
LANES = 128
VMEM = pl.BlockSpec(memory_space=pltpu.VMEM)
HBM = pl.BlockSpec(memory_space=pltpu.HBM)


def swapped(x, axis, first):
    count = lax.axis_size(axis)
    pairs = []
    for low in range(first, first + count, 2):
        a, b = low % count, (low + 1) % count
        pairs += [(a, b), (b, a)]
    return lax.ppermute(x, axis, pairs)


def moved(x, target_of):
    times, spaces = lax.axis_size("tm"), lax.axis_size("space")
    pairs = []
    for t in range(times):
        target = target_of(t)
        for s in range(spaces):
            pairs.append((t * spaces + s, target * spaces + (s if target > t else s ^ 1)))
    return lax.ppermute(x, ("tm", "space"), pairs)


def in_hbm(x):
    return pltpu.with_memory_space_constraint(x, pltpu.HBM)


def copies_of(sources, targets, sems):
    return [pltpu.make_async_copy(s, t, sems.at[i]) for i, (s, t) in enumerate(zip(sources, targets))]


def stage_kernel(*refs):
    count = len(refs) // 2
    copies = copies_of(refs[:count], refs[count:-1], refs[-1])
    early = lax.axis_index("tm") <= 1

    @pl.when(early)
    def _():
        copies[-1].start()

    for copy in copies[:-1]:
        copy.start()
    for copy in copies[:-1]:
        copy.wait()

    @pl.when(early)
    def _():
        copies[-1].wait()


def pack_kernel(odd_ref, even_ref, own_ref, packed_ref):
    space, count = lax.axis_index("space"), lax.axis_size("space")
    frames, rows, cols, width = own_ref.shape
    is_even = lax.rem(space, 2) == 0
    even, odd = even_ref[...], odd_ref[...]
    above = jnp.where(space > 0, jnp.where(is_even, odd, even), jnp.zeros_like(even))
    below = jnp.where(space < count - 1, jnp.where(is_even, even, odd), jnp.zeros_like(even))
    channel = lax.broadcasted_iota(jnp.int32, (width, LANES), 0)
    lane = lax.broadcasted_iota(jnp.int32, (width, LANES), 1)
    total = jnp.zeros((frames * cols, LANES), jnp.float32)
    for r, block in enumerate([x[:, r] for x in (above, own_ref[...], below) for r in range(rows)]):
        spread = (lane == channel + r * width).astype(own_ref.dtype)
        total += jnp.dot(block.reshape(frames * cols, width), spread, preferred_element_type=jnp.float32)
    packed_ref[...] = total.astype(own_ref.dtype).reshape(packed_ref.shape)


def column_shift(x, by, cols):
    groups = x.shape[0] // cols
    column = lax.broadcasted_iota(jnp.int32, (groups, cols, x.shape[1]), 1).reshape(x.shape)
    edge = 0 if by > 0 else cols - 1
    return jnp.where(column == edge, 0.0, pltpu.roll(x, by % x.shape[0], axis=0))


def column_taps(frames, rows, width):
    frame_total, cols, _ = frames.shape
    tall = rows + 2
    reach = 3 * width
    flat = frames.astype(jnp.float32).reshape(frame_total * cols, LANES)
    lane = lax.broadcasted_iota(jnp.int32, flat.shape, 1)
    west, east = column_shift(flat, 1, cols), column_shift(flat, -1, cols)
    later = jnp.concatenate([east[cols:], east[:cols]], axis=0)

    def window(x, r, at):
        return pltpu.roll(x, (at - r * width) % LANES, axis=1) if at != r * width else x

    def by_position(x, y):
        parts = [jnp.where(lane < reach, window(x, r, 0), window(y, r, reach)) for r in range(tall)]
        parts = [part.astype(jnp.bfloat16).reshape(frame_total, cols, LANES) for part in parts]
        return jnp.stack(parts, axis=1).reshape(frame_total * tall * cols, LANES)

    return by_position(west, flat), by_position(east, later)


def weight_taps(w_in_ref, width, taps):
    rows = [
        w_in_ref[((a * 3 + b) * 3 + e) * width : ((a * 3 + b) * 3 + e + 1) * width, :] for a, e in taps for b in range(3)
    ]
    return rows + [jnp.zeros((LANES - len(rows) * width, w_in_ref.shape[1]), jnp.bfloat16)]


def entry(frames, w_in_ref, b_in_ref, rows, width):
    pair, last = column_taps(frames, rows, width)
    block = (rows + 2) * frames.shape[1]
    size = (frames.shape[0] - 2) * block
    left = [pair[a * block : a * block + size] for a in range(3)] + [last[:size], last[2 * block : 2 * block + size]]
    right = []
    for taps in [[(a, 0), (a, 1)] for a in range(3)] + [[(0, 2), (1, 2)], [(2, 2)]]:
        right += weight_taps(w_in_ref, width, taps)
    left, right = jnp.concatenate(left, axis=1), jnp.concatenate(right, axis=0)
    return jnp.dot(left, right, preferred_element_type=jnp.float32) + b_in_ref[...][None, :]


def normalized(hidden, gain_ref):
    inverse = lax.rsqrt(jnp.mean(hidden * hidden, axis=1, keepdims=True) + EPSILON)
    half = hidden * inverse * (0.5 * gain_ref[...][None, :])
    return (half + half * jnp.tanh(half)).astype(jnp.bfloat16)


def own_part(active, w_time_ref):
    features = active.shape[1]
    block = active.shape[0] // 2
    early, late = active[:block], active[block:]
    left = jnp.concatenate(
        [jnp.concatenate([jnp.zeros_like(early), early], axis=1), jnp.concatenate([early, late], axis=1)], axis=0
    )
    return jnp.dot(left, w_time_ref[features:, :], preferred_element_type=jnp.float32)


def finish(frames, w_in_ref, b_in_ref, gain_ref, b_time_ref, b_up_ref, w_time_ref, taps_ref, out_ref, scratch, rows, width):
    cols = frames.shape[1]
    active = normalized(entry(frames, w_in_ref, b_in_ref, rows, width), gain_ref)
    block = (rows + 2) * cols
    left = jnp.concatenate([active[a * block : (a + 2) * block] for a in range(3)], axis=1)
    timed = jnp.dot(left, w_time_ref[...], preferred_element_type=jnp.float32) + b_time_ref[...][None, :]
    upsample(timed, taps_ref, b_up_ref, out_ref, *scratch, rows, cols)


def prepare_taps(w_up_ref, taps_ref):
    features = w_up_ref.shape[1]
    out_width = taps_ref.shape[-1]
    for e in range(3):
        taps = [w_up_ref[(b * 3 + e) * out_width : (b * 3 + e + 1) * out_width, :].T for b in range(3)]
        top, middle, bottom = (x.astype(jnp.float32) for x in taps)
        taps_ref[0, e, :features] = taps[0]
        taps_ref[0, e, features:] = (middle + bottom).astype(taps_ref.dtype)
        taps_ref[1, e, :features] = (top + middle).astype(taps_ref.dtype)
        taps_ref[1, e, features:] = taps[2]


def upsample(timed, taps_ref, b_up_ref, out_ref, wide_ref, done_ref, sems, rows, cols):
    space, space_count = lax.axis_index("space"), lax.axis_size("space")
    features = timed.shape[1] // 2
    tall = rows + 2
    frames = timed.shape[0] // (tall * cols)
    out_width = done_ref.shape[-1]
    timed = timed.astype(jnp.bfloat16)

    def timed_row(f, h, r):
        x = timed[(f * tall + r) * cols : (f * tall + r + 1) * cols, h * features : (h + 1) * features]
        if r == 0:
            x = jnp.where(space > 0, x, jnp.zeros_like(x))
        if r == tall - 1:
            x = jnp.where(space < space_count - 1, x, jnp.zeros_like(x))
        return x

    doubled = [[timed_row(f, h, r) for r in range(tall)] for f in range(frames) for h in range(2)]
    copies = []
    for p in range(2):
        left = jnp.concatenate(
            [jnp.concatenate([frame[r + p + k] for frame in doubled for r in range(rows)], axis=0) for k in range(2)], axis=1
        )
        sums = [jnp.dot(left, taps_ref[p, e], preferred_element_type=jnp.float32) for e in range(3)]
        middle = sums[1] + b_up_ref[...][None, :]
        even = column_shift(sums[0], 1, cols) + (middle + sums[2])
        odd = column_shift(sums[2], -1, cols) + (middle + sums[0])
        half = even.shape[0]
        for q, x in enumerate((even, odd)):
            wide_ref[p, 0, pl.ds(q, half, stride=2), :] = x[:, :LANES]
            wide_ref[p, 1, pl.ds(q, half, stride=2), pl.ds(0, out_width - LANES)] = x[:, LANES:]
        low, high = wide_ref[p, 0], wide_ref[p, 1, :, pl.ds(0, out_width - LANES)]
        place = done_ref.shape[1:-1]
        done_ref[p, :, :, :, :LANES] = low.astype(done_ref.dtype).reshape(place + (LANES,))
        done_ref[p, :, :, :, LANES:] = high.astype(done_ref.dtype).reshape(place + (out_width - LANES,))
        copies.append(pltpu.make_async_copy(done_ref.at[p], out_ref.at[:, :, p], sems.at[p]))
        copies[-1].start()
    for copy in copies:
        copy.wait()


def first_kernel(
    own_ref, w_in_ref, b_in_ref, gain_ref, b_time_ref, b_up_ref, w_up_ref, w_time_hbm, _w_time,
    out_ref, w_time_ref, taps_ref, wide_ref, done_ref, sems, *, rows, width,
):
    time = lax.axis_index("tm")

    @pl.when(time == 0)
    def _():
        prepare_taps(w_up_ref, taps_ref)
        own = own_ref[...]
        hidden = entry(jnp.concatenate([jnp.zeros_like(own), own], axis=0), w_in_ref, b_in_ref, rows, width)
        timed = own_part(normalized(hidden, gain_ref), w_time_ref) + b_time_ref[...][None, :]
        upsample(timed, taps_ref, b_up_ref, out_ref, wide_ref, done_ref, sems, rows, own.shape[1])

    @pl.when(time > 1)
    def _():
        copy = pltpu.make_async_copy(w_time_hbm, w_time_ref, sems.at[0])
        copy.start()
        prepare_taps(w_up_ref, taps_ref)
        copy.wait()

    @pl.when(time == 1)
    def _():
        prepare_taps(w_up_ref, taps_ref)


def second_kernel(
    own_ref, one_ref, w_in_ref, b_in_ref, gain_ref, b_time_ref, b_up_ref, w_time_ref, taps_ref, _out,
    out_ref, *scratch, rows, width,
):
    @pl.when(lax.axis_index("tm") == 1)
    def _():
        frames = jnp.concatenate([jnp.zeros_like(one_ref), one_ref[...], own_ref[...]], axis=0)
        finish(frames, w_in_ref, b_in_ref, gain_ref, b_time_ref, b_up_ref, w_time_ref, taps_ref, out_ref, scratch, rows, width)


def last_kernel(
    own_ref, two_ref, one_ref, w_in_ref, b_in_ref, gain_ref, b_time_ref, b_up_ref, w_time_ref, taps_ref, _out,
    out_ref, *scratch, rows, width,
):
    @pl.when(lax.axis_index("tm") > 1)
    def _():
        frames = jnp.concatenate([two_ref[...], one_ref[...], own_ref[...]], axis=0)
        finish(frames, w_in_ref, b_in_ref, gain_ref, b_time_ref, b_up_ref, w_time_ref, taps_ref, out_ref, scratch, rows, width)


def params(mib):
    return pltpu.CompilerParams(vmem_limit_bytes=mib * 1024 * 1024)


def shards(latent, w_in, b_in, gain_in, w_time, b_time, w_up, b_up):
    frames, rows, cols, width = latent.shape
    features = w_in.shape[-1]
    out_width = w_up.shape[-1]
    w_time = in_hbm(w_time.reshape(-1, w_time.shape[-1]))
    w_up = in_hbm(jnp.swapaxes(w_up, 2, 3).reshape(-1, w_up.shape[2]))
    out_shape = (2 * frames, rows, 2, 2 * cols, out_width)

    even = swapped(latent, "space", 0)
    odd = swapped(latent, "space", 1)
    arrays = [in_hbm(x) for x in (w_in.reshape(-1, features), b_in, gain_in, b_time, b_up, latent)] + [w_up, w_time]
    w_in, b_in, gain_in, b_time, b_up, own, w_up, w_time_kept = pl.pallas_call(
        stage_kernel,
        out_shape=[pltpu.VMEM(x.shape, x.dtype) for x in arrays],
        in_specs=[HBM] * len(arrays),
        out_specs=[VMEM] * len(arrays),
        scratch_shapes=[pltpu.SemaphoreType.DMA((len(arrays),))],
        compiler_params=params(1),
    )(*arrays)
    taps_shape = pltpu.VMEM((2, 3, 2 * features, out_width), jnp.bfloat16)
    own = pl.pallas_call(
        pack_kernel,
        out_shape=pltpu.VMEM((frames, cols, LANES), latent.dtype),
        in_specs=[VMEM] * 3,
        out_specs=VMEM,
        compiler_params=params(1),
    )(odd, even, own)
    times = lax.axis_size("tm")
    first = moved(own, lambda t: (1 - t) % times if t < 2 else t)
    two = moved(own, lambda t: (t + 2) % times)
    one = moved(own, lambda t: t if t == 0 else t % (times - 1) + 1)

    scratch = [
        pltpu.VMEM((2, 2, 2 * frames * rows * 2 * cols, LANES), jnp.float32),
        pltpu.VMEM((2, 2 * frames, rows, 2 * cols, out_width), jnp.bfloat16),
        pltpu.SemaphoreType.DMA((2,)),
    ]
    result = pltpu.HBM(out_shape, jnp.bfloat16)
    out, w_time_kept, taps = pl.pallas_call(
        functools.partial(first_kernel, rows=rows, width=width),
        out_shape=[result, pltpu.VMEM(w_time.shape, w_time.dtype), taps_shape],
        in_specs=[VMEM] * 7 + [HBM, VMEM],
        out_specs=[HBM] + [VMEM] * 2,
        scratch_shapes=scratch,
        input_output_aliases={8: 1},
        compiler_params=params(16),
    )(own, w_in, b_in, gain_in, b_time, b_up, w_up, w_time, w_time_kept)
    out = pl.pallas_call(
        functools.partial(second_kernel, rows=rows, width=width),
        out_shape=result,
        in_specs=[VMEM] * 9 + [HBM],
        out_specs=HBM,
        scratch_shapes=scratch,
        input_output_aliases={9: 0},
        compiler_params=params(16),
    )(own, first, w_in, b_in, gain_in, b_time, b_up, w_time_kept, taps, out)
    out = pl.pallas_call(
        functools.partial(last_kernel, rows=rows, width=width),
        out_shape=result,
        in_specs=[VMEM] * 10 + [HBM],
        out_specs=HBM,
        scratch_shapes=scratch,
        input_output_aliases={10: 0},
        compiler_params=params(16),
    )(own, two, one, w_in, b_in, gain_in, b_time, b_up, w_time_kept, taps, out)
    return out.reshape(2 * frames, 2 * rows, 2 * cols, out_width)


def solution(mesh):
    in_specs = (P(("clips", "tm"), "space", None, None), P(), P(), P(), P(), P(), P(), P())
    out_specs = P(("clips", "tm"), "space", None, None)
    return jax.shard_map(shards, mesh=mesh, in_specs=in_specs, out_specs=out_specs, check_vma=False)
```

```python
import functools

import jax
import jax.numpy as jnp
from jax import lax
from jax.experimental import pallas as pl
from jax.experimental.pallas import tpu as pltpu
from jax.sharding import PartitionSpec as P

EPSILON = 1e-06
LANES = 128
VMEM = pl.BlockSpec(memory_space=pltpu.VMEM)
HBM = pl.BlockSpec(memory_space=pltpu.HBM)


def swapped(x, axis, first):
    count = lax.axis_size(axis)
    pairs = []
    for low in range(first, first + count, 2):
        a, b = low % count, (low + 1) % count
        pairs += [(a, b), (b, a)]
    return lax.ppermute(x, axis, pairs)


def moved(x, target_of):
    times, spaces = lax.axis_size("tm"), lax.axis_size("space")
    pairs = []
    for t in range(times):
        target = target_of(t)
        for s in range(spaces):
            pairs.append((t * spaces + s, target * spaces + (s if target > t else s ^ 1)))
    return lax.ppermute(x, ("tm", "space"), pairs)


def in_hbm(x):
    return pltpu.with_memory_space_constraint(x, pltpu.HBM)


def copies_of(sources, targets, sems):
    return [pltpu.make_async_copy(s, t, sems.at[i]) for i, (s, t) in enumerate(zip(sources, targets))]


def stage_kernel(*refs):
    count = len(refs) // 2
    copies = copies_of(refs[:count], refs[count:-1], refs[-1])
    for copy in copies:
        copy.start()
    for copy in copies:
        copy.wait()


def pack_kernel(odd_ref, even_ref, own_ref, packed_ref):
    space, count = lax.axis_index("space"), lax.axis_size("space")
    frames, rows, cols, width = own_ref.shape
    is_even = lax.rem(space, 2) == 0
    even, odd = even_ref[...], odd_ref[...]
    above = jnp.where(space > 0, jnp.where(is_even, odd, even), jnp.zeros_like(even))
    below = jnp.where(space < count - 1, jnp.where(is_even, even, odd), jnp.zeros_like(even))
    channel = lax.broadcasted_iota(jnp.int32, (width, LANES), 0)
    lane = lax.broadcasted_iota(jnp.int32, (width, LANES), 1)
    total = jnp.zeros((frames * cols, LANES), jnp.float32)
    for r, block in enumerate([x[:, r] for x in (above, own_ref[...], below) for r in range(rows)]):
        spread = (lane == channel + r * width).astype(own_ref.dtype)
        total += jnp.dot(block.reshape(frames * cols, width), spread, preferred_element_type=jnp.float32)
    packed_ref[...] = total.astype(own_ref.dtype).reshape(packed_ref.shape)


def column_shift(x, by, cols):
    groups = x.shape[0] // cols
    column = lax.broadcasted_iota(jnp.int32, (groups, cols, x.shape[1]), 1).reshape(x.shape)
    edge = 0 if by > 0 else cols - 1
    return jnp.where(column == edge, 0.0, pltpu.roll(x, by % x.shape[0], axis=0))


def column_taps(frames, rows, width):
    frame_total, cols, _ = frames.shape
    tall = rows + 2
    reach = 3 * width
    flat = frames.astype(jnp.float32).reshape(frame_total * cols, LANES)
    lane = lax.broadcasted_iota(jnp.int32, flat.shape, 1)
    west, east = column_shift(flat, 1, cols), column_shift(flat, -1, cols)
    later = jnp.concatenate([east[cols:], east[:cols]], axis=0)

    def window(x, r, at):
        return pltpu.roll(x, (at - r * width) % LANES, axis=1) if at != r * width else x

    def by_position(x, y):
        parts = [jnp.where(lane < reach, window(x, r, 0), window(y, r, reach)) for r in range(tall)]
        parts = [part.astype(jnp.bfloat16).reshape(frame_total, cols, LANES) for part in parts]
        return jnp.stack(parts, axis=1).reshape(frame_total * tall * cols, LANES)

    return by_position(west, flat), by_position(east, later)


def weight_taps(w_in_ref, width, taps):
    rows = [
        w_in_ref[((a * 3 + b) * 3 + e) * width : ((a * 3 + b) * 3 + e + 1) * width, :] for a, e in taps for b in range(3)
    ]
    return rows + [jnp.zeros((LANES - len(rows) * width, w_in_ref.shape[1]), jnp.bfloat16)]


def entry(frames, w_in_ref, b_in_ref, rows, width):
    pair, last = column_taps(frames, rows, width)
    block = (rows + 2) * frames.shape[1]
    size = (frames.shape[0] - 2) * block
    left = [pair[a * block : a * block + size] for a in range(3)] + [last[:size], last[2 * block : 2 * block + size]]
    right = []
    for taps in [[(a, 0), (a, 1)] for a in range(3)] + [[(0, 2), (1, 2)], [(2, 2)]]:
        right += weight_taps(w_in_ref, width, taps)
    left, right = jnp.concatenate(left, axis=1), jnp.concatenate(right, axis=0)
    return jnp.dot(left, right, preferred_element_type=jnp.float32) + b_in_ref[...][None, :]


def normalized(hidden, gain_ref):
    inverse = lax.rsqrt(jnp.mean(hidden * hidden, axis=1, keepdims=True) + EPSILON)
    half = hidden * inverse * (0.5 * gain_ref[...][None, :])
    return (half + half * jnp.tanh(half)).astype(jnp.bfloat16)


def finish(frames, w_in_ref, b_in_ref, gain_ref, b_time_ref, b_up_ref, w_time_ref, taps_ref, out_ref, scratch, rows, width):
    cols = frames.shape[1]
    features = w_in_ref.shape[1]
    active = normalized(entry(frames, w_in_ref, b_in_ref, rows, width), gain_ref)
    block = (rows + 2) * cols
    if frames.shape[0] == 4:
        early, late = active[:block], active[block:]
        left = [jnp.concatenate([jnp.zeros_like(early), early], axis=0), active]
        w_time = w_time_ref[features:, :]
    else:
        left = [active[a * block : (a + 2) * block] for a in range(3)]
        w_time = w_time_ref[...]
    timed = jnp.dot(jnp.concatenate(left, axis=1), w_time, preferred_element_type=jnp.float32)
    upsample(timed + b_time_ref[...][None, :], taps_ref, b_up_ref, out_ref, *scratch, rows, cols)


def prepare_taps(w_up_ref, taps_ref):
    features = w_up_ref.shape[1]
    out_width = taps_ref.shape[-1]
    for e in range(3):
        taps = [w_up_ref[(b * 3 + e) * out_width : (b * 3 + e + 1) * out_width, :].T for b in range(3)]
        top, middle, bottom = (x.astype(jnp.float32) for x in taps)
        taps_ref[0, e, :features] = taps[0]
        taps_ref[0, e, features:] = (middle + bottom).astype(taps_ref.dtype)
        taps_ref[1, e, :features] = (top + middle).astype(taps_ref.dtype)
        taps_ref[1, e, features:] = taps[2]


def upsample(timed, taps_ref, b_up_ref, out_ref, wide_ref, done_ref, sems, rows, cols):
    space, space_count = lax.axis_index("space"), lax.axis_size("space")
    features = timed.shape[1] // 2
    tall = rows + 2
    frames = timed.shape[0] // (tall * cols)
    out_width = done_ref.shape[-1]
    timed = timed.astype(jnp.bfloat16)

    def timed_row(f, h, r):
        x = timed[(f * tall + r) * cols : (f * tall + r + 1) * cols, h * features : (h + 1) * features]
        if r == 0:
            x = jnp.where(space > 0, x, jnp.zeros_like(x))
        if r == tall - 1:
            x = jnp.where(space < space_count - 1, x, jnp.zeros_like(x))
        return x

    doubled = [[timed_row(f, h, r) for r in range(tall)] for f in range(frames) for h in range(2)]
    copies = []
    for p in range(2):
        left = jnp.concatenate(
            [jnp.concatenate([frame[r + p + k] for frame in doubled for r in range(rows)], axis=0) for k in range(2)], axis=1
        )
        sums = [jnp.dot(left, taps_ref[p, e], preferred_element_type=jnp.float32) for e in range(3)]
        middle = sums[1] + b_up_ref[...][None, :]
        even = column_shift(sums[0], 1, cols) + (middle + sums[2])
        odd = column_shift(sums[2], -1, cols) + (middle + sums[0])
        half = even.shape[0]
        for q, x in enumerate((even, odd)):
            wide_ref[p, 0, pl.ds(q, half, stride=2), :] = x[:, :LANES]
            wide_ref[p, 1, pl.ds(q, half, stride=2), pl.ds(0, out_width - LANES)] = x[:, LANES:]
        low, high = wide_ref[p, 0], wide_ref[p, 1, :, pl.ds(0, out_width - LANES)]
        place = done_ref.shape[1:-1]
        done_ref[p, :, :, :, :LANES] = low.astype(done_ref.dtype).reshape(place + (LANES,))
        done_ref[p, :, :, :, LANES:] = high.astype(done_ref.dtype).reshape(place + (out_width - LANES,))
        copies.append(pltpu.make_async_copy(done_ref.at[p], out_ref.at[:, :, p], sems.at[p]))
        copies[-1].start()
    for copy in copies:
        copy.wait()


def first_kernel(
    own_ref, w_in_ref, b_in_ref, gain_ref, b_time_ref, b_up_ref, w_time_ref, w_up_ref, out_ref, taps_ref, *scratch, rows, width
):
    time = lax.axis_index("tm")

    @pl.when(time == 0)
    def _():
        prepare_taps(w_up_ref, taps_ref)
        frames = jnp.concatenate([jnp.zeros_like(own_ref), own_ref[...]], axis=0)
        finish(frames, w_in_ref, b_in_ref, gain_ref, b_time_ref, b_up_ref, w_time_ref, taps_ref, out_ref, scratch, rows, width)

    @pl.when(time > 0)
    def _():
        prepare_taps(w_up_ref, taps_ref)


def second_kernel(
    own_ref, one_ref, w_in_ref, b_in_ref, gain_ref, b_time_ref, b_up_ref, w_time_ref, taps_ref, _out,
    out_ref, *scratch, rows, width,
):
    @pl.when(lax.axis_index("tm") == 1)
    def _():
        frames = jnp.concatenate([jnp.zeros_like(one_ref), one_ref[...], own_ref[...]], axis=0)
        finish(frames, w_in_ref, b_in_ref, gain_ref, b_time_ref, b_up_ref, w_time_ref, taps_ref, out_ref, scratch, rows, width)


def last_kernel(
    own_ref, two_ref, one_ref, w_in_ref, b_in_ref, gain_ref, b_time_ref, b_up_ref, w_time_ref, taps_ref, _out,
    out_ref, *scratch, rows, width,
):
    @pl.when(lax.axis_index("tm") > 1)
    def _():
        frames = jnp.concatenate([two_ref[...], one_ref[...], own_ref[...]], axis=0)
        finish(frames, w_in_ref, b_in_ref, gain_ref, b_time_ref, b_up_ref, w_time_ref, taps_ref, out_ref, scratch, rows, width)


def params(mib):
    return pltpu.CompilerParams(vmem_limit_bytes=mib * 1024 * 1024)


def shards(latent, w_in, b_in, gain_in, w_time, b_time, w_up, b_up):
    frames, rows, cols, width = latent.shape
    features = w_in.shape[-1]
    out_width = w_up.shape[-1]
    w_time = in_hbm(w_time.reshape(-1, w_time.shape[-1]))
    w_up = in_hbm(jnp.swapaxes(w_up, 2, 3).reshape(-1, w_up.shape[2]))
    out_shape = (2 * frames, rows, 2, 2 * cols, out_width)

    even = swapped(latent, "space", 0)
    odd = swapped(latent, "space", 1)
    arrays = [w_time, w_up] + [in_hbm(x) for x in (w_in.reshape(-1, features), b_in, gain_in, b_time, b_up, latent)]
    w_time, w_up, w_in, b_in, gain_in, b_time, b_up, own = pl.pallas_call(
        stage_kernel,
        out_shape=[pltpu.VMEM(x.shape, x.dtype) for x in arrays],
        in_specs=[HBM] * len(arrays),
        out_specs=[VMEM] * len(arrays),
        scratch_shapes=[pltpu.SemaphoreType.DMA((len(arrays),))],
        compiler_params=params(1),
    )(*arrays)
    own = pl.pallas_call(
        pack_kernel,
        out_shape=pltpu.VMEM((frames, cols, LANES), latent.dtype),
        in_specs=[VMEM] * 3,
        out_specs=VMEM,
        compiler_params=params(1),
    )(odd, even, own)
    times = lax.axis_size("tm")
    first = moved(own, lambda t: (1 - t) % times if t < 2 else t)
    two = moved(own, lambda t: (t + 2) % times)
    one = moved(own, lambda t: t if t == 0 else t % (times - 1) + 1)

    scratch = [
        pltpu.VMEM((2, 2, 2 * frames * rows * 2 * cols, LANES), jnp.float32),
        pltpu.VMEM((2, 2 * frames, rows, 2 * cols, out_width), jnp.bfloat16),
        pltpu.SemaphoreType.DMA((2,)),
    ]
    result = pltpu.HBM(out_shape, jnp.bfloat16)
    out, taps = pl.pallas_call(
        functools.partial(first_kernel, rows=rows, width=width),
        out_shape=[result, pltpu.VMEM((2, 3, 2 * features, out_width), jnp.bfloat16)],
        in_specs=[VMEM] * 8,
        out_specs=[HBM, VMEM],
        scratch_shapes=scratch,
        compiler_params=params(16),
    )(own, w_in, b_in, gain_in, b_time, b_up, w_time, w_up)
    out = pl.pallas_call(
        functools.partial(second_kernel, rows=rows, width=width),
        out_shape=result,
        in_specs=[VMEM] * 9 + [HBM],
        out_specs=HBM,
        scratch_shapes=scratch,
        input_output_aliases={9: 0},
        compiler_params=params(16),
    )(own, first, w_in, b_in, gain_in, b_time, b_up, w_time, taps, out)
    out = pl.pallas_call(
        functools.partial(last_kernel, rows=rows, width=width),
        out_shape=result,
        in_specs=[VMEM] * 10 + [HBM],
        out_specs=HBM,
        scratch_shapes=scratch,
        input_output_aliases={10: 0},
        compiler_params=params(16),
    )(own, two, one, w_in, b_in, gain_in, b_time, b_up, w_time, taps, out)
    return out.reshape(2 * frames, 2 * rows, 2 * cols, out_width)


def solution(mesh):
    in_specs = (P(("clips", "tm"), "space", None, None), P(), P(), P(), P(), P(), P(), P())
    out_specs = P(("clips", "tm"), "space", None, None)
    return jax.shard_map(shards, mesh=mesh, in_specs=in_specs, out_specs=out_specs, check_vma=False)
```

```python
import functools

import jax
import jax.numpy as jnp
from jax import lax
from jax.experimental import pallas as pl
from jax.experimental.pallas import tpu as pltpu
from jax.sharding import PartitionSpec as P

EPSILON = 1e-06
LANES = 128
VMEM = pl.BlockSpec(memory_space=pltpu.VMEM)
HBM = pl.BlockSpec(memory_space=pltpu.HBM)


def swapped(x, axis, first):
    count = lax.axis_size(axis)
    pairs = []
    for low in range(first, first + count, 2):
        a, b = low % count, (low + 1) % count
        pairs += [(a, b), (b, a)]
    return lax.ppermute(x, axis, pairs)


def moved(x, target_of):
    times, spaces = lax.axis_size("tm"), lax.axis_size("space")
    pairs = []
    for t in range(times):
        target = target_of(t)
        for s in range(spaces):
            pairs.append((t * spaces + s, target * spaces + (s ^ 1 if target == t or t - target > 1 else s)))
    return lax.ppermute(x, ("tm", "space"), pairs)


def in_hbm(x):
    return pltpu.with_memory_space_constraint(x, pltpu.HBM)


def copies_of(sources, targets, sems):
    return [pltpu.make_async_copy(s, t, sems.at[i]) for i, (s, t) in enumerate(zip(sources, targets))]


def stage_kernel(*refs):
    count = len(refs) // 2
    copies = copies_of(refs[:count], refs[count:-1], refs[-1])
    for copy in copies:
        copy.start()
    for copy in copies:
        copy.wait()


def pack_kernel(odd_ref, even_ref, own_ref, packed_ref):
    space, count = lax.axis_index("space"), lax.axis_size("space")
    frames, rows, cols, width = own_ref.shape
    is_even = lax.rem(space, 2) == 0
    even, odd = even_ref[...], odd_ref[...]
    above = jnp.where(space > 0, jnp.where(is_even, odd, even), jnp.zeros_like(even))
    below = jnp.where(space < count - 1, jnp.where(is_even, even, odd), jnp.zeros_like(even))
    channel = lax.broadcasted_iota(jnp.int32, (width, LANES), 0)
    lane = lax.broadcasted_iota(jnp.int32, (width, LANES), 1)
    total = jnp.zeros((frames * cols, LANES), jnp.float32)
    for r, block in enumerate([x[:, r] for x in (above, own_ref[...], below) for r in range(rows)]):
        spread = (lane == channel + r * width).astype(own_ref.dtype)
        total += jnp.dot(block.reshape(frames * cols, width), spread, preferred_element_type=jnp.float32)
    packed_ref[...] = total.astype(own_ref.dtype).reshape(packed_ref.shape)


def column_shift(x, by, cols):
    groups = x.shape[0] // cols
    column = lax.broadcasted_iota(jnp.int32, (groups, cols, x.shape[1]), 1).reshape(x.shape)
    edge = 0 if by > 0 else cols - 1
    return jnp.where(column == edge, 0.0, pltpu.roll(x, by % x.shape[0], axis=0))


def column_taps(frames, rows, width):
    frame_total, cols, _ = frames.shape
    tall = rows + 2
    reach = 3 * width
    flat = frames.astype(jnp.float32).reshape(frame_total * cols, LANES)
    lane = lax.broadcasted_iota(jnp.int32, flat.shape, 1)
    west, east = column_shift(flat, 1, cols), column_shift(flat, -1, cols)
    later = jnp.concatenate([east[cols:], east[:cols]], axis=0)

    def window(x, r, at):
        return pltpu.roll(x, (at - r * width) % LANES, axis=1) if at != r * width else x

    def by_position(x, y):
        parts = [jnp.where(lane < reach, window(x, r, 0), window(y, r, reach)) for r in range(tall)]
        parts = [part.astype(jnp.bfloat16).reshape(frame_total, cols, LANES) for part in parts]
        return jnp.stack(parts, axis=1).reshape(frame_total * tall * cols, LANES)

    return by_position(west, flat), by_position(east, later)


def weight_taps(w_in_ref, width, taps):
    rows = [
        w_in_ref[((a * 3 + b) * 3 + e) * width : ((a * 3 + b) * 3 + e + 1) * width, :] for a, e in taps for b in range(3)
    ]
    return rows + [jnp.zeros((LANES - len(rows) * width, w_in_ref.shape[1]), jnp.bfloat16)]


def entry(frames, w_in_ref, b_in_ref, rows, width):
    pair, last = column_taps(frames, rows, width)
    block = (rows + 2) * frames.shape[1]
    size = (frames.shape[0] - 2) * block
    left = [pair[a * block : a * block + size] for a in range(3)] + [last[:size], last[2 * block : 2 * block + size]]
    right = []
    for taps in [[(a, 0), (a, 1)] for a in range(3)] + [[(0, 2), (1, 2)], [(2, 2)]]:
        right += weight_taps(w_in_ref, width, taps)
    left, right = jnp.concatenate(left, axis=1), jnp.concatenate(right, axis=0)
    return jnp.dot(left, right, preferred_element_type=jnp.float32) + b_in_ref[...][None, :]


def normalized(hidden, gain_ref):
    inverse = lax.rsqrt(jnp.mean(hidden * hidden, axis=1, keepdims=True) + EPSILON)
    half = hidden * inverse * (0.5 * gain_ref[...][None, :])
    return (half + half * jnp.tanh(half)).astype(jnp.bfloat16)


def finish(frames, w_in_ref, b_in_ref, gain_ref, b_time_ref, b_up_ref, w_time_ref, taps_ref, out_ref, scratch, rows, width):
    cols = frames.shape[1]
    features = w_in_ref.shape[1]
    active = normalized(entry(frames, w_in_ref, b_in_ref, rows, width), gain_ref)
    block = (rows + 2) * cols
    if frames.shape[0] == 4:
        early, late = active[:block], active[block:]
        left = [jnp.concatenate([jnp.zeros_like(early), early], axis=0), active]
        w_time = w_time_ref[features:, :]
    else:
        left = [active[a * block : (a + 2) * block] for a in range(3)]
        w_time = w_time_ref[...]
    timed = jnp.dot(jnp.concatenate(left, axis=1), w_time, preferred_element_type=jnp.float32)
    upsample(timed + b_time_ref[...][None, :], taps_ref, b_up_ref, out_ref, *scratch, rows, cols)


def prepare_taps(w_up_ref, taps_ref):
    features = w_up_ref.shape[1]
    out_width = taps_ref.shape[-1]
    for e in range(3):
        taps = [w_up_ref[(b * 3 + e) * out_width : (b * 3 + e + 1) * out_width, :].T for b in range(3)]
        top, middle, bottom = (x.astype(jnp.float32) for x in taps)
        taps_ref[0, e, :features] = taps[0]
        taps_ref[0, e, features:] = (middle + bottom).astype(taps_ref.dtype)
        taps_ref[1, e, :features] = (top + middle).astype(taps_ref.dtype)
        taps_ref[1, e, features:] = taps[2]


def upsample(timed, taps_ref, b_up_ref, out_ref, wide_ref, done_ref, sems, rows, cols):
    space, space_count = lax.axis_index("space"), lax.axis_size("space")
    features = timed.shape[1] // 2
    tall = rows + 2
    frames = timed.shape[0] // (tall * cols)
    out_width = done_ref.shape[-1]
    timed = timed.astype(jnp.bfloat16)

    def timed_row(f, h, r):
        x = timed[(f * tall + r) * cols : (f * tall + r + 1) * cols, h * features : (h + 1) * features]
        if r == 0:
            x = jnp.where(space > 0, x, jnp.zeros_like(x))
        if r == tall - 1:
            x = jnp.where(space < space_count - 1, x, jnp.zeros_like(x))
        return x

    doubled = [[timed_row(f, h, r) for r in range(tall)] for f in range(frames) for h in range(2)]
    copies = []
    for p in range(2):
        left = jnp.concatenate(
            [jnp.concatenate([frame[r + p + k] for frame in doubled for r in range(rows)], axis=0) for k in range(2)], axis=1
        )
        sums = [jnp.dot(left, taps_ref[p, e], preferred_element_type=jnp.float32) for e in range(3)]
        middle = sums[1] + b_up_ref[...][None, :]
        even = column_shift(sums[0], 1, cols) + (middle + sums[2])
        odd = column_shift(sums[2], -1, cols) + (middle + sums[0])
        half = even.shape[0]
        for q, x in enumerate((even, odd)):
            wide_ref[p, 0, pl.ds(q, half, stride=2), :] = x[:, :LANES]
            wide_ref[p, 1, pl.ds(q, half, stride=2), pl.ds(0, out_width - LANES)] = x[:, LANES:]
        low, high = wide_ref[p, 0], wide_ref[p, 1, :, pl.ds(0, out_width - LANES)]
        place = done_ref.shape[1:-1]
        done_ref[p, :, :, :, :LANES] = low.astype(done_ref.dtype).reshape(place + (LANES,))
        done_ref[p, :, :, :, LANES:] = high.astype(done_ref.dtype).reshape(place + (out_width - LANES,))
        copies.append(pltpu.make_async_copy(done_ref.at[p], out_ref.at[:, :, p], sems.at[p]))
        copies[-1].start()
    for copy in copies:
        copy.wait()


def first_kernel(
    own_ref, w_in_ref, b_in_ref, gain_ref, b_time_ref, b_up_ref, w_time_ref, w_up_ref, out_ref, taps_ref, *scratch, rows, width
):
    time = lax.axis_index("tm")

    @pl.when(time == 0)
    def _():
        prepare_taps(w_up_ref, taps_ref)
        frames = jnp.concatenate([jnp.zeros_like(own_ref), own_ref[...]], axis=0)
        finish(frames, w_in_ref, b_in_ref, gain_ref, b_time_ref, b_up_ref, w_time_ref, taps_ref, out_ref, scratch, rows, width)

    @pl.when(time > 0)
    def _():
        prepare_taps(w_up_ref, taps_ref)


def second_kernel(
    own_ref, one_ref, w_in_ref, b_in_ref, gain_ref, b_time_ref, b_up_ref, w_time_ref, taps_ref, _out,
    out_ref, *scratch, rows, width,
):
    @pl.when(lax.axis_index("tm") == 1)
    def _():
        frames = jnp.concatenate([jnp.zeros_like(one_ref), one_ref[...], own_ref[...]], axis=0)
        finish(frames, w_in_ref, b_in_ref, gain_ref, b_time_ref, b_up_ref, w_time_ref, taps_ref, out_ref, scratch, rows, width)


def third_kernel(
    own_ref, near_ref, two_ref, w_in_ref, b_in_ref, gain_ref, b_time_ref, b_up_ref, w_time_ref, taps_ref, _out,
    out_ref, *scratch, rows, width, mine,
):
    @pl.when(mine(lax.axis_index("tm")))
    def _():
        frames = jnp.concatenate([two_ref[...], near_ref[...], own_ref[...]], axis=0)
        finish(frames, w_in_ref, b_in_ref, gain_ref, b_time_ref, b_up_ref, w_time_ref, taps_ref, out_ref, scratch, rows, width)


def params(mib):
    return pltpu.CompilerParams(vmem_limit_bytes=mib * 1024 * 1024)


def shards(latent, w_in, b_in, gain_in, w_time, b_time, w_up, b_up):
    frames, rows, cols, width = latent.shape
    features = w_in.shape[-1]
    out_width = w_up.shape[-1]
    w_time = in_hbm(w_time.reshape(-1, w_time.shape[-1]))
    w_up = in_hbm(jnp.swapaxes(w_up, 2, 3).reshape(-1, w_up.shape[2]))
    out_shape = (2 * frames, rows, 2, 2 * cols, out_width)

    even = swapped(latent, "space", 0)
    odd = swapped(latent, "space", 1)
    arrays = [w_time, w_up] + [in_hbm(x) for x in (w_in.reshape(-1, features), b_in, gain_in, b_time, b_up, latent)]
    w_time, w_up, w_in, b_in, gain_in, b_time, b_up, own = pl.pallas_call(
        stage_kernel,
        out_shape=[pltpu.VMEM(x.shape, x.dtype) for x in arrays],
        in_specs=[HBM] * len(arrays),
        out_specs=[VMEM] * len(arrays),
        scratch_shapes=[pltpu.SemaphoreType.DMA((len(arrays),))],
        compiler_params=params(1),
    )(*arrays)
    own = pl.pallas_call(
        pack_kernel,
        out_shape=pltpu.VMEM((frames, cols, LANES), latent.dtype),
        in_specs=[VMEM] * 3,
        out_specs=VMEM,
        compiler_params=params(1),
    )(odd, even, own)
    times = lax.axis_size("tm")
    first = moved(own, lambda t: (t + 1) % min(3, times) if t < 3 else t)
    two = moved(own, lambda t: (t + 2) % times)
    one = moved(own, lambda t: t if t < 2 else (t - 1) % (times - 2) + 2)

    scratch = [
        pltpu.VMEM((2, 2, 2 * frames * rows * 2 * cols, LANES), jnp.float32),
        pltpu.VMEM((2, 2 * frames, rows, 2 * cols, out_width), jnp.bfloat16),
        pltpu.SemaphoreType.DMA((2,)),
    ]
    result = pltpu.HBM(out_shape, jnp.bfloat16)
    out, taps = pl.pallas_call(
        functools.partial(first_kernel, rows=rows, width=width),
        out_shape=[result, pltpu.VMEM((2, 3, 2 * features, out_width), jnp.bfloat16)],
        in_specs=[VMEM] * 8,
        out_specs=[HBM, VMEM],
        scratch_shapes=scratch,
        compiler_params=params(16),
    )(own, w_in, b_in, gain_in, b_time, b_up, w_time, w_up)
    out = pl.pallas_call(
        functools.partial(second_kernel, rows=rows, width=width),
        out_shape=result,
        in_specs=[VMEM] * 9 + [HBM],
        out_specs=HBM,
        scratch_shapes=scratch,
        input_output_aliases={9: 0},
        compiler_params=params(16),
    )(own, first, w_in, b_in, gain_in, b_time, b_up, w_time, taps, out)
    for near, mine in ((first, lambda time: time == 2), (one, lambda time: time > 2)):
        out = pl.pallas_call(
            functools.partial(third_kernel, rows=rows, width=width, mine=mine),
            out_shape=result,
            in_specs=[VMEM] * 10 + [HBM],
            out_specs=HBM,
            scratch_shapes=scratch,
            input_output_aliases={10: 0},
            compiler_params=params(16),
        )(own, near, two, w_in, b_in, gain_in, b_time, b_up, w_time, taps, out)
    return out.reshape(2 * frames, 2 * rows, 2 * cols, out_width)


def solution(mesh):
    in_specs = (P(("clips", "tm"), "space", None, None), P(), P(), P(), P(), P(), P(), P())
    out_specs = P(("clips", "tm"), "space", None, None)
    return jax.shard_map(shards, mesh=mesh, in_specs=in_specs, out_specs=out_specs, check_vma=False)
```

```python
import functools

import jax
import jax.numpy as jnp
from jax import lax
from jax.experimental import pallas as pl
from jax.experimental.pallas import tpu as pltpu
from jax.sharding import PartitionSpec as P

EPSILON = 1e-06
LANES = 128
VMEM = pl.BlockSpec(memory_space=pltpu.VMEM)
HBM = pl.BlockSpec(memory_space=pltpu.HBM)


def swapped(x, axis, first):
    count = lax.axis_size(axis)
    pairs = []
    for low in range(first, first + count, 2):
        a, b = low % count, (low + 1) % count
        pairs += [(a, b), (b, a)]
    return lax.ppermute(x, axis, pairs)


def moved(x, target_of):
    times, spaces = lax.axis_size("tm"), lax.axis_size("space")
    pairs = []
    for t in range(times):
        target = target_of(t)
        for s in range(spaces):
            pairs.append((t * spaces + s, target * spaces + (s ^ 1 if target == t or t - target > 1 else s)))
    return lax.ppermute(x, ("tm", "space"), pairs)


def in_hbm(x):
    return pltpu.with_memory_space_constraint(x, pltpu.HBM)


def copies_of(sources, targets, sems):
    return [pltpu.make_async_copy(s, t, sems.at[i]) for i, (s, t) in enumerate(zip(sources, targets))]


def stage_kernel(*refs):
    count = len(refs) // 2
    copies = copies_of(refs[:count], refs[count:-1], refs[-1])
    for copy in copies:
        copy.start()
    for copy in copies:
        copy.wait()


def pack_kernel(odd_ref, even_ref, own_ref, packed_ref):
    space, count = lax.axis_index("space"), lax.axis_size("space")
    frames, rows, cols, width = own_ref.shape
    is_even = lax.rem(space, 2) == 0
    even, odd = even_ref[...], odd_ref[...]
    above = jnp.where(space > 0, jnp.where(is_even, odd, even), jnp.zeros_like(even))
    below = jnp.where(space < count - 1, jnp.where(is_even, even, odd), jnp.zeros_like(even))
    pieces = [x[:, r].reshape(frames * cols, width) for x in (above, own_ref[...], below) for r in range(rows)]
    blank = jnp.zeros((frames * cols, LANES - 3 * rows * width), packed_ref.dtype)
    packed_ref[...] = jnp.concatenate(pieces + [blank], axis=1).reshape(packed_ref.shape)


def column_shift(x, by, cols):
    groups = x.shape[0] // cols
    column = lax.broadcasted_iota(jnp.int32, (groups, cols, x.shape[1]), 1).reshape(x.shape)
    edge = 0 if by > 0 else cols - 1
    return jnp.where(column == edge, 0.0, pltpu.roll(x, by % x.shape[0], axis=0))


def column_taps(frames, rows, width):
    frame_total, cols, _ = frames.shape
    tall = rows + 2
    reach = 3 * width
    flat = frames.astype(jnp.float32).reshape(frame_total * cols, LANES)
    lane = lax.broadcasted_iota(jnp.int32, flat.shape, 1)
    west, east = column_shift(flat, 1, cols), column_shift(flat, -1, cols)
    later = jnp.concatenate([east[cols:], east[:cols]], axis=0)

    def window(x, r, at):
        return pltpu.roll(x, (at - r * width) % LANES, axis=1) if at != r * width else x

    def by_position(x, y):
        parts = [jnp.where(lane < reach, window(x, r, 0), window(y, r, reach)) for r in range(tall)]
        parts = [part.astype(jnp.bfloat16).reshape(frame_total, cols, LANES) for part in parts]
        return jnp.stack(parts, axis=1).reshape(frame_total * tall * cols, LANES)

    return by_position(west, flat), by_position(east, later)


def weight_taps(w_in_ref, width, taps):
    rows = [
        w_in_ref[((a * 3 + b) * 3 + e) * width : ((a * 3 + b) * 3 + e + 1) * width, :] for a, e in taps for b in range(3)
    ]
    return rows + [jnp.zeros((LANES - len(rows) * width, w_in_ref.shape[1]), jnp.bfloat16)]


def entry(frames, w_in_ref, b_in_ref, rows, width):
    pair, last = column_taps(frames, rows, width)
    block = (rows + 2) * frames.shape[1]
    size = (frames.shape[0] - 2) * block
    left = [pair[a * block : a * block + size] for a in range(3)] + [last[:size], last[2 * block : 2 * block + size]]
    right = []
    for taps in [[(a, 0), (a, 1)] for a in range(3)] + [[(0, 2), (1, 2)], [(2, 2)]]:
        right += weight_taps(w_in_ref, width, taps)
    left, right = jnp.concatenate(left, axis=1), jnp.concatenate(right, axis=0)
    return jnp.dot(left, right, preferred_element_type=jnp.float32) + b_in_ref[...][None, :]


def normalized(hidden, gain_ref):
    inverse = lax.rsqrt(jnp.mean(hidden * hidden, axis=1, keepdims=True) + EPSILON)
    half = hidden * inverse * (0.5 * gain_ref[...][None, :])
    return (half + half * jnp.tanh(half)).astype(jnp.bfloat16)


def finish(frames, w_in_ref, b_in_ref, gain_ref, b_time_ref, b_up_ref, w_time_ref, taps_ref, out_ref, scratch, rows, width):
    cols = frames.shape[1]
    features = w_in_ref.shape[1]
    active = normalized(entry(frames, w_in_ref, b_in_ref, rows, width), gain_ref)
    block = (rows + 2) * cols
    if frames.shape[0] == 4:
        early, late = active[:block], active[block:]
        left = [jnp.concatenate([jnp.zeros_like(early), early], axis=0), active]
        w_time = w_time_ref[features:, :]
    else:
        left = [active[a * block : (a + 2) * block] for a in range(3)]
        w_time = w_time_ref[...]
    timed = jnp.dot(jnp.concatenate(left, axis=1), w_time, preferred_element_type=jnp.float32)
    upsample(timed + b_time_ref[...][None, :], taps_ref, b_up_ref, out_ref, *scratch, rows, cols)


def prepare_taps(w_up_ref, taps_ref):
    features = w_up_ref.shape[1]
    out_width = taps_ref.shape[-1]
    for e in range(3):
        taps = [w_up_ref[(b * 3 + e) * out_width : (b * 3 + e + 1) * out_width, :].T for b in range(3)]
        top, middle, bottom = (x.astype(jnp.float32) for x in taps)
        taps_ref[0, e, :features] = taps[0]
        taps_ref[0, e, features:] = (middle + bottom).astype(taps_ref.dtype)
        taps_ref[1, e, :features] = (top + middle).astype(taps_ref.dtype)
        taps_ref[1, e, features:] = taps[2]


def upsample(timed, taps_ref, b_up_ref, out_ref, wide_ref, done_ref, sems, rows, cols):
    space, space_count = lax.axis_index("space"), lax.axis_size("space")
    features = timed.shape[1] // 2
    tall = rows + 2
    frames = timed.shape[0] // (tall * cols)
    out_width = done_ref.shape[-1]
    timed = timed.astype(jnp.bfloat16)

    def timed_row(f, h, r):
        x = timed[(f * tall + r) * cols : (f * tall + r + 1) * cols, h * features : (h + 1) * features]
        if r == 0:
            x = jnp.where(space > 0, x, jnp.zeros_like(x))
        if r == tall - 1:
            x = jnp.where(space < space_count - 1, x, jnp.zeros_like(x))
        return x

    doubled = [[timed_row(f, h, r) for r in range(tall)] for f in range(frames) for h in range(2)]
    copies = []
    for p in range(2):
        left = jnp.concatenate(
            [jnp.concatenate([frame[r + p + k] for frame in doubled for r in range(rows)], axis=0) for k in range(2)], axis=1
        )
        sums = [jnp.dot(left, taps_ref[p, e], preferred_element_type=jnp.float32) for e in range(3)]
        middle = sums[1] + b_up_ref[...][None, :]
        even = column_shift(sums[0], 1, cols) + (middle + sums[2])
        odd = column_shift(sums[2], -1, cols) + (middle + sums[0])
        half = even.shape[0]
        for q, x in enumerate((even, odd)):
            wide_ref[p, 0, pl.ds(q, half, stride=2), :] = x[:, :LANES]
            wide_ref[p, 1, pl.ds(q, half, stride=2), pl.ds(0, out_width - LANES)] = x[:, LANES:]
        low, high = wide_ref[p, 0], wide_ref[p, 1, :, pl.ds(0, out_width - LANES)]
        place = done_ref.shape[1:-1]
        done_ref[p, :, :, :, :LANES] = low.astype(done_ref.dtype).reshape(place + (LANES,))
        done_ref[p, :, :, :, LANES:] = high.astype(done_ref.dtype).reshape(place + (out_width - LANES,))
        copies.append(pltpu.make_async_copy(done_ref.at[p], out_ref.at[:, :, p], sems.at[p]))
        copies[-1].start()
    for copy in copies:
        copy.wait()


def first_kernel(
    own_ref, w_in_ref, b_in_ref, gain_ref, b_time_ref, b_up_ref, w_time_ref, w_up_ref, out_ref, taps_ref, *scratch, rows, width
):
    time = lax.axis_index("tm")

    @pl.when(time == 0)
    def _():
        prepare_taps(w_up_ref, taps_ref)
        frames = jnp.concatenate([jnp.zeros_like(own_ref), own_ref[...]], axis=0)
        finish(frames, w_in_ref, b_in_ref, gain_ref, b_time_ref, b_up_ref, w_time_ref, taps_ref, out_ref, scratch, rows, width)

    @pl.when(time > 0)
    def _():
        prepare_taps(w_up_ref, taps_ref)


def second_kernel(
    own_ref, one_ref, w_in_ref, b_in_ref, gain_ref, b_time_ref, b_up_ref, w_time_ref, taps_ref, _out,
    out_ref, *scratch, rows, width,
):
    @pl.when(lax.axis_index("tm") == 1)
    def _():
        frames = jnp.concatenate([jnp.zeros_like(one_ref), one_ref[...], own_ref[...]], axis=0)
        finish(frames, w_in_ref, b_in_ref, gain_ref, b_time_ref, b_up_ref, w_time_ref, taps_ref, out_ref, scratch, rows, width)


def third_kernel(
    own_ref, near_ref, two_ref, w_in_ref, b_in_ref, gain_ref, b_time_ref, b_up_ref, w_time_ref, taps_ref, _out,
    out_ref, *scratch, rows, width, mine,
):
    @pl.when(mine(lax.axis_index("tm")))
    def _():
        frames = jnp.concatenate([two_ref[...], near_ref[...], own_ref[...]], axis=0)
        finish(frames, w_in_ref, b_in_ref, gain_ref, b_time_ref, b_up_ref, w_time_ref, taps_ref, out_ref, scratch, rows, width)


def params(mib):
    return pltpu.CompilerParams(vmem_limit_bytes=mib * 1024 * 1024)


def shards(latent, w_in, b_in, gain_in, w_time, b_time, w_up, b_up):
    frames, rows, cols, width = latent.shape
    features = w_in.shape[-1]
    out_width = w_up.shape[-1]
    w_time = in_hbm(w_time.reshape(-1, w_time.shape[-1]))
    w_up = in_hbm(jnp.swapaxes(w_up, 2, 3).reshape(-1, w_up.shape[2]))
    out_shape = (2 * frames, rows, 2, 2 * cols, out_width)

    even = swapped(latent, "space", 0)
    odd = swapped(latent, "space", 1)
    arrays = [w_time, w_up] + [in_hbm(x) for x in (w_in.reshape(-1, features), b_in, gain_in, b_time, b_up, latent)]
    w_time, w_up, w_in, b_in, gain_in, b_time, b_up, own = pl.pallas_call(
        stage_kernel,
        out_shape=[pltpu.VMEM(x.shape, x.dtype) for x in arrays],
        in_specs=[HBM] * len(arrays),
        out_specs=[VMEM] * len(arrays),
        scratch_shapes=[pltpu.SemaphoreType.DMA((len(arrays),))],
        compiler_params=params(1),
    )(*arrays)
    own = pl.pallas_call(
        pack_kernel,
        out_shape=pltpu.VMEM((frames, cols, LANES), latent.dtype),
        in_specs=[VMEM] * 3,
        out_specs=VMEM,
        compiler_params=params(1),
    )(odd, even, own)
    times = lax.axis_size("tm")
    first = moved(own, lambda t: (t + 1) % min(3, times) if t < 3 else t)
    two = moved(own, lambda t: (t + 2) % times)
    one = moved(own, lambda t: t if t < 2 else (t - 1) % (times - 2) + 2)

    scratch = [
        pltpu.VMEM((2, 2, 2 * frames * rows * 2 * cols, LANES), jnp.float32),
        pltpu.VMEM((2, 2 * frames, rows, 2 * cols, out_width), jnp.bfloat16),
        pltpu.SemaphoreType.DMA((2,)),
    ]
    result = pltpu.HBM(out_shape, jnp.bfloat16)
    out, taps = pl.pallas_call(
        functools.partial(first_kernel, rows=rows, width=width),
        out_shape=[result, pltpu.VMEM((2, 3, 2 * features, out_width), jnp.bfloat16)],
        in_specs=[VMEM] * 8,
        out_specs=[HBM, VMEM],
        scratch_shapes=scratch,
        compiler_params=params(16),
    )(own, w_in, b_in, gain_in, b_time, b_up, w_time, w_up)
    out = pl.pallas_call(
        functools.partial(second_kernel, rows=rows, width=width),
        out_shape=result,
        in_specs=[VMEM] * 9 + [HBM],
        out_specs=HBM,
        scratch_shapes=scratch,
        input_output_aliases={9: 0},
        compiler_params=params(16),
    )(own, first, w_in, b_in, gain_in, b_time, b_up, w_time, taps, out)
    for near, mine in ((first, lambda time: time == 2), (one, lambda time: time > 2)):
        out = pl.pallas_call(
            functools.partial(third_kernel, rows=rows, width=width, mine=mine),
            out_shape=result,
            in_specs=[VMEM] * 10 + [HBM],
            out_specs=HBM,
            scratch_shapes=scratch,
            input_output_aliases={10: 0},
            compiler_params=params(16),
        )(own, near, two, w_in, b_in, gain_in, b_time, b_up, w_time, taps, out)
    return out.reshape(2 * frames, 2 * rows, 2 * cols, out_width)


def solution(mesh):
    in_specs = (P(("clips", "tm"), "space", None, None), P(), P(), P(), P(), P(), P(), P())
    out_specs = P(("clips", "tm"), "space", None, None)
    return jax.shard_map(shards, mesh=mesh, in_specs=in_specs, out_specs=out_specs, check_vma=False)
```

```python
import functools

import jax
import jax.numpy as jnp
from jax import lax
from jax.experimental import pallas as pl
from jax.experimental.pallas import tpu as pltpu
from jax.sharding import PartitionSpec as P

EPSILON = 1e-06
LANES = 128
VMEM = pl.BlockSpec(memory_space=pltpu.VMEM)
HBM = pl.BlockSpec(memory_space=pltpu.HBM)


def swapped(x, axis, first):
    count = lax.axis_size(axis)
    pairs = []
    for low in range(first, first + count, 2):
        a, b = low % count, (low + 1) % count
        pairs += [(a, b), (b, a)]
    return lax.ppermute(x, axis, pairs)


def moved(x, target_of):
    times, spaces = lax.axis_size("tm"), lax.axis_size("space")
    pairs = []
    for t in range(times):
        target = target_of(t)
        for s in range(spaces):
            pairs.append((t * spaces + s, target * spaces + (s ^ 1 if target == t or t - target > 1 else s)))
    return lax.ppermute(x, ("tm", "space"), pairs)


def in_hbm(x):
    return pltpu.with_memory_space_constraint(x, pltpu.HBM)


def copies_of(sources, targets, sems):
    return [pltpu.make_async_copy(s, t, sems.at[i]) for i, (s, t) in enumerate(zip(sources, targets))]


def stage_kernel(*refs):
    count = len(refs) // 2
    copies = copies_of(refs[:count], refs[count:-1], refs[-1])
    for copy in copies:
        copy.start()
    for copy in copies:
        copy.wait()


def pack_kernel(odd_ref, even_ref, own_ref, packed_ref):
    space, count = lax.axis_index("space"), lax.axis_size("space")
    frames, rows, cols, width = own_ref.shape
    is_even = lax.rem(space, 2) == 0
    even, odd = even_ref[...], odd_ref[...]
    above = jnp.where(space > 0, jnp.where(is_even, odd, even), jnp.zeros_like(even))
    below = jnp.where(space < count - 1, jnp.where(is_even, even, odd), jnp.zeros_like(even))
    pieces = [x[:, r].reshape(frames * cols, width) for x in (above, own_ref[...], below) for r in range(rows)]
    blank = jnp.zeros((frames * cols, LANES - 3 * rows * width), packed_ref.dtype)
    packed_ref[...] = jnp.concatenate(pieces + [blank], axis=1).reshape(packed_ref.shape)


def column_shift(x, by, cols):
    groups = x.shape[0] // cols
    column = lax.broadcasted_iota(jnp.int32, (groups, cols, x.shape[1]), 1).reshape(x.shape)
    edge = 0 if by > 0 else cols - 1
    return jnp.where(column == edge, 0.0, pltpu.roll(x, by % x.shape[0], axis=0))


def column_taps(frames, rows, width):
    frame_total, cols, _ = frames.shape
    tall = rows + 2
    reach = 3 * width
    flat = frames.astype(jnp.float32).reshape(frame_total * cols, LANES)
    lane = lax.broadcasted_iota(jnp.int32, flat.shape, 1)
    west, east = column_shift(flat, 1, cols), column_shift(flat, -1, cols)
    later = jnp.concatenate([east[cols:], east[:cols]], axis=0)

    def window(x, r, at):
        return pltpu.roll(x, (at - r * width) % LANES, axis=1) if at != r * width else x

    def by_position(x, y):
        parts = [jnp.where(lane < reach, window(x, r, 0), window(y, r, reach)) for r in range(tall)]
        parts = [part.astype(jnp.bfloat16).reshape(frame_total, cols, LANES) for part in parts]
        return jnp.stack(parts, axis=1).reshape(frame_total * tall * cols, LANES)

    return by_position(west, flat), by_position(east, later)


def weight_taps(w_in_ref, width, taps):
    rows = [
        w_in_ref[((a * 3 + b) * 3 + e) * width : ((a * 3 + b) * 3 + e + 1) * width, :] for a, e in taps for b in range(3)
    ]
    return rows + [jnp.zeros((LANES - len(rows) * width, w_in_ref.shape[1]), jnp.bfloat16)]


def entry(frames, w_in_ref, b_in_ref, rows, width):
    pair, last = column_taps(frames, rows, width)
    block = (rows + 2) * frames.shape[1]
    size = (frames.shape[0] - 2) * block
    left = [pair[a * block : a * block + size] for a in range(3)] + [last[:size], last[2 * block : 2 * block + size]]
    right = []
    for taps in [[(a, 0), (a, 1)] for a in range(3)] + [[(0, 2), (1, 2)], [(2, 2)]]:
        right += weight_taps(w_in_ref, width, taps)
    left, right = jnp.concatenate(left, axis=1), jnp.concatenate(right, axis=0)
    return jnp.dot(left, right, preferred_element_type=jnp.float32) + b_in_ref[...][None, :]


def normalized(hidden, gain_ref):
    inverse = lax.rsqrt(jnp.mean(hidden * hidden, axis=1, keepdims=True) + EPSILON)
    half = hidden * inverse * (0.5 * gain_ref[...][None, :])
    return (half + half * jnp.tanh(half)).astype(jnp.bfloat16)


def finish(frames, w_in_ref, b_in_ref, gain_ref, b_time_ref, b_up_ref, w_time_ref, taps_ref, out_ref, scratch, rows, width):
    cols = frames.shape[1]
    features = w_in_ref.shape[1]
    active = normalized(entry(frames, w_in_ref, b_in_ref, rows, width), gain_ref)
    block = (rows + 2) * cols
    if frames.shape[0] == 4:
        early, late = active[:block], active[block:]
        left = [jnp.concatenate([jnp.zeros_like(early), early], axis=0), active]
        w_time = w_time_ref[features:, :]
    else:
        left = [active[a * block : (a + 2) * block] for a in range(3)]
        w_time = w_time_ref[...]
    left = jnp.concatenate(left, axis=1)
    halves = [jnp.dot(left, w_time[:, n : n + features], preferred_element_type=jnp.float32) for n in (0, features)]
    timed = jnp.concatenate(halves, axis=1)
    upsample(timed + b_time_ref[...][None, :], taps_ref, b_up_ref, out_ref, *scratch, rows, cols)


def prepare_taps(w_up_ref, taps_ref):
    features = w_up_ref.shape[1]
    out_width = taps_ref.shape[-1]
    for e in range(3):
        taps = [w_up_ref[(b * 3 + e) * out_width : (b * 3 + e + 1) * out_width, :].T for b in range(3)]
        top, middle, bottom = (x.astype(jnp.float32) for x in taps)
        taps_ref[0, e, :features] = taps[0]
        taps_ref[0, e, features:] = (middle + bottom).astype(taps_ref.dtype)
        taps_ref[1, e, :features] = (top + middle).astype(taps_ref.dtype)
        taps_ref[1, e, features:] = taps[2]


def upsample(timed, taps_ref, b_up_ref, out_ref, wide_ref, done_ref, sems, rows, cols):
    space, space_count = lax.axis_index("space"), lax.axis_size("space")
    features = timed.shape[1] // 2
    tall = rows + 2
    frames = timed.shape[0] // (tall * cols)
    out_width = done_ref.shape[-1]
    timed = timed.astype(jnp.bfloat16)

    def timed_row(f, h, r):
        x = timed[(f * tall + r) * cols : (f * tall + r + 1) * cols, h * features : (h + 1) * features]
        if r == 0:
            x = jnp.where(space > 0, x, jnp.zeros_like(x))
        if r == tall - 1:
            x = jnp.where(space < space_count - 1, x, jnp.zeros_like(x))
        return x

    doubled = [[timed_row(f, h, r) for r in range(tall)] for f in range(frames) for h in range(2)]
    copies = []
    for p in range(2):
        left = jnp.concatenate(
            [jnp.concatenate([frame[r + p + k] for frame in doubled for r in range(rows)], axis=0) for k in range(2)], axis=1
        )
        sums = [jnp.dot(left, taps_ref[p, e], preferred_element_type=jnp.float32) for e in range(3)]
        middle = sums[1] + b_up_ref[...][None, :]
        even = column_shift(sums[0], 1, cols) + (middle + sums[2])
        odd = column_shift(sums[2], -1, cols) + (middle + sums[0])
        half = even.shape[0]
        for q, x in enumerate((even, odd)):
            wide_ref[p, 0, pl.ds(q, half, stride=2), :] = x[:, :LANES]
            wide_ref[p, 1, pl.ds(q, half, stride=2), pl.ds(0, out_width - LANES)] = x[:, LANES:]
        low, high = wide_ref[p, 0], wide_ref[p, 1, :, pl.ds(0, out_width - LANES)]
        place = done_ref.shape[1:-1]
        done_ref[p, :, :, :, :LANES] = low.astype(done_ref.dtype).reshape(place + (LANES,))
        done_ref[p, :, :, :, LANES:] = high.astype(done_ref.dtype).reshape(place + (out_width - LANES,))
        copies.append(pltpu.make_async_copy(done_ref.at[p], out_ref.at[:, :, p], sems.at[p]))
        copies[-1].start()
    for copy in copies:
        copy.wait()


def first_kernel(
    own_ref, w_in_ref, b_in_ref, gain_ref, b_time_ref, b_up_ref, w_time_ref, w_up_ref, out_ref, taps_ref, *scratch, rows, width
):
    time = lax.axis_index("tm")

    @pl.when(time == 0)
    def _():
        prepare_taps(w_up_ref, taps_ref)
        frames = jnp.concatenate([jnp.zeros_like(own_ref), own_ref[...]], axis=0)
        finish(frames, w_in_ref, b_in_ref, gain_ref, b_time_ref, b_up_ref, w_time_ref, taps_ref, out_ref, scratch, rows, width)

    @pl.when(time > 0)
    def _():
        prepare_taps(w_up_ref, taps_ref)


def second_kernel(
    own_ref, one_ref, w_in_ref, b_in_ref, gain_ref, b_time_ref, b_up_ref, w_time_ref, taps_ref, _out,
    out_ref, *scratch, rows, width,
):
    @pl.when(lax.axis_index("tm") == 1)
    def _():
        frames = jnp.concatenate([jnp.zeros_like(one_ref), one_ref[...], own_ref[...]], axis=0)
        finish(frames, w_in_ref, b_in_ref, gain_ref, b_time_ref, b_up_ref, w_time_ref, taps_ref, out_ref, scratch, rows, width)


def third_kernel(
    own_ref, near_ref, two_ref, w_in_ref, b_in_ref, gain_ref, b_time_ref, b_up_ref, w_time_ref, taps_ref, _out,
    out_ref, *scratch, rows, width, mine,
):
    @pl.when(mine(lax.axis_index("tm")))
    def _():
        frames = jnp.concatenate([two_ref[...], near_ref[...], own_ref[...]], axis=0)
        finish(frames, w_in_ref, b_in_ref, gain_ref, b_time_ref, b_up_ref, w_time_ref, taps_ref, out_ref, scratch, rows, width)


def params(mib):
    return pltpu.CompilerParams(vmem_limit_bytes=mib * 1024 * 1024)


def shards(latent, w_in, b_in, gain_in, w_time, b_time, w_up, b_up):
    frames, rows, cols, width = latent.shape
    features = w_in.shape[-1]
    out_width = w_up.shape[-1]
    w_time = in_hbm(w_time.reshape(-1, w_time.shape[-1]))
    w_up = in_hbm(jnp.swapaxes(w_up, 2, 3).reshape(-1, w_up.shape[2]))
    out_shape = (2 * frames, rows, 2, 2 * cols, out_width)

    even = swapped(latent, "space", 0)
    odd = swapped(latent, "space", 1)
    arrays = [w_time, w_up] + [in_hbm(x) for x in (w_in.reshape(-1, features), b_in, gain_in, b_time, b_up, latent)]
    w_time, w_up, w_in, b_in, gain_in, b_time, b_up, own = pl.pallas_call(
        stage_kernel,
        out_shape=[pltpu.VMEM(x.shape, x.dtype) for x in arrays],
        in_specs=[HBM] * len(arrays),
        out_specs=[VMEM] * len(arrays),
        scratch_shapes=[pltpu.SemaphoreType.DMA((len(arrays),))],
        compiler_params=params(1),
    )(*arrays)
    own = pl.pallas_call(
        pack_kernel,
        out_shape=pltpu.VMEM((frames, cols, LANES), latent.dtype),
        in_specs=[VMEM] * 3,
        out_specs=VMEM,
        compiler_params=params(1),
    )(odd, even, own)
    times = lax.axis_size("tm")
    first = moved(own, lambda t: (t + 1) % min(3, times) if t < 3 else t)
    two = moved(own, lambda t: (t + 2) % times)
    one = moved(own, lambda t: t if t < 2 else (t - 1) % (times - 2) + 2)

    scratch = [
        pltpu.VMEM((2, 2, 2 * frames * rows * 2 * cols, LANES), jnp.float32),
        pltpu.VMEM((2, 2 * frames, rows, 2 * cols, out_width), jnp.bfloat16),
        pltpu.SemaphoreType.DMA((2,)),
    ]
    result = pltpu.HBM(out_shape, jnp.bfloat16)
    out, taps = pl.pallas_call(
        functools.partial(first_kernel, rows=rows, width=width),
        out_shape=[result, pltpu.VMEM((2, 3, 2 * features, out_width), jnp.bfloat16)],
        in_specs=[VMEM] * 8,
        out_specs=[HBM, VMEM],
        scratch_shapes=scratch,
        compiler_params=params(16),
    )(own, w_in, b_in, gain_in, b_time, b_up, w_time, w_up)
    out = pl.pallas_call(
        functools.partial(second_kernel, rows=rows, width=width),
        out_shape=result,
        in_specs=[VMEM] * 9 + [HBM],
        out_specs=HBM,
        scratch_shapes=scratch,
        input_output_aliases={9: 0},
        compiler_params=params(16),
    )(own, first, w_in, b_in, gain_in, b_time, b_up, w_time, taps, out)
    for near, mine in ((first, lambda time: time == 2), (one, lambda time: time > 2)):
        out = pl.pallas_call(
            functools.partial(third_kernel, rows=rows, width=width, mine=mine),
            out_shape=result,
            in_specs=[VMEM] * 10 + [HBM],
            out_specs=HBM,
            scratch_shapes=scratch,
            input_output_aliases={10: 0},
            compiler_params=params(16),
        )(own, near, two, w_in, b_in, gain_in, b_time, b_up, w_time, taps, out)
    return out.reshape(2 * frames, 2 * rows, 2 * cols, out_width)


def solution(mesh):
    in_specs = (P(("clips", "tm"), "space", None, None), P(), P(), P(), P(), P(), P(), P())
    out_specs = P(("clips", "tm"), "space", None, None)
    return jax.shard_map(shards, mesh=mesh, in_specs=in_specs, out_specs=out_specs, check_vma=False)
```

```python
import functools

import jax
import jax.numpy as jnp
from jax import lax
from jax.experimental import pallas as pl
from jax.experimental.pallas import tpu as pltpu
from jax.sharding import PartitionSpec as P

EPSILON = 1e-06
LANES = 128
VMEM = pl.BlockSpec(memory_space=pltpu.VMEM)
HBM = pl.BlockSpec(memory_space=pltpu.HBM)


def swapped(x, axis, first):
    count = lax.axis_size(axis)
    pairs = []
    for low in range(first, first + count, 2):
        a, b = low % count, (low + 1) % count
        pairs += [(a, b), (b, a)]
    return lax.ppermute(x, axis, pairs)


def moved(x, target_of):
    times, spaces = lax.axis_size("tm"), lax.axis_size("space")
    pairs = []
    for t in range(times):
        for s in range(spaces):
            target, tile = target_of(t, s)
            pairs.append((t * spaces + s, target * spaces + tile))
    return lax.ppermute(x, ("tm", "space"), pairs)


def in_hbm(x):
    return pltpu.with_memory_space_constraint(x, pltpu.HBM)


def copies_of(sources, targets, sems):
    return [pltpu.make_async_copy(s, t, sems.at[i]) for i, (s, t) in enumerate(zip(sources, targets))]


def stage_kernel(*refs):
    count = len(refs) // 2
    copies = copies_of(refs[:count], refs[count:-1], refs[-1])
    for copy in copies:
        copy.start()
    for copy in copies:
        copy.wait()


def pack_kernel(odd_ref, even_ref, own_ref, packed_ref):
    space, count = lax.axis_index("space"), lax.axis_size("space")
    frames, rows, cols, width = own_ref.shape
    is_even = lax.rem(space, 2) == 0
    even, odd = even_ref[...], odd_ref[...]
    above = jnp.where(space > 0, jnp.where(is_even, odd, even), jnp.zeros_like(even))
    below = jnp.where(space < count - 1, jnp.where(is_even, even, odd), jnp.zeros_like(even))
    pieces = [x[:, r].reshape(frames * cols, width) for x in (above, own_ref[...], below) for r in range(rows)]
    blank = jnp.zeros((frames * cols, LANES - 3 * rows * width), packed_ref.dtype)
    packed_ref[...] = jnp.concatenate(pieces + [blank], axis=1).reshape(packed_ref.shape)


def column_shift(x, by, cols):
    groups = x.shape[0] // cols
    column = lax.broadcasted_iota(jnp.int32, (groups, cols, x.shape[1]), 1).reshape(x.shape)
    edge = 0 if by > 0 else cols - 1
    return jnp.where(column == edge, 0.0, pltpu.roll(x, by % x.shape[0], axis=0))


def column_taps(frames, rows, width):
    frame_total, cols, _ = frames.shape
    tall = rows + 2
    reach = 3 * width
    flat = frames.astype(jnp.float32).reshape(frame_total * cols, LANES)
    lane = lax.broadcasted_iota(jnp.int32, flat.shape, 1)
    west, east = column_shift(flat, 1, cols), column_shift(flat, -1, cols)
    later = jnp.concatenate([east[cols:], east[:cols]], axis=0)

    def window(x, r, at):
        return pltpu.roll(x, (at - r * width) % LANES, axis=1) if at != r * width else x

    def by_position(x, y):
        parts = [jnp.where(lane < reach, window(x, r, 0), window(y, r, reach)) for r in range(tall)]
        parts = [part.astype(jnp.bfloat16).reshape(frame_total, cols, LANES) for part in parts]
        return jnp.stack(parts, axis=1).reshape(frame_total * tall * cols, LANES)

    return by_position(west, flat), by_position(east, later)


def weight_taps(w_in_ref, width, taps):
    rows = [
        w_in_ref[((a * 3 + b) * 3 + e) * width : ((a * 3 + b) * 3 + e + 1) * width, :] for a, e in taps for b in range(3)
    ]
    return rows + [jnp.zeros((LANES - len(rows) * width, w_in_ref.shape[1]), jnp.bfloat16)]


def entry(frames, w_in_ref, b_in_ref, rows, width):
    pair, last = column_taps(frames, rows, width)
    block = (rows + 2) * frames.shape[1]
    size = (frames.shape[0] - 2) * block
    left = [pair[a * block : a * block + size] for a in range(3)] + [last[:size], last[2 * block : 2 * block + size]]
    right = []
    for taps in [[(a, 0), (a, 1)] for a in range(3)] + [[(0, 2), (1, 2)], [(2, 2)]]:
        right += weight_taps(w_in_ref, width, taps)
    left, right = jnp.concatenate(left, axis=1), jnp.concatenate(right, axis=0)
    return jnp.dot(left, right, preferred_element_type=jnp.float32) + b_in_ref[...][None, :]


def normalized(hidden, gain_ref):
    inverse = lax.rsqrt(jnp.mean(hidden * hidden, axis=1, keepdims=True) + EPSILON)
    half = hidden * inverse * (0.5 * gain_ref[...][None, :])
    return (half + half * jnp.tanh(half)).astype(jnp.bfloat16)


def finish(frames, w_in_ref, b_in_ref, gain_ref, b_time_ref, b_up_ref, w_time_ref, taps_ref, out_ref, scratch, rows, width):
    cols = frames.shape[1]
    features = w_in_ref.shape[1]
    active = normalized(entry(frames, w_in_ref, b_in_ref, rows, width), gain_ref)
    block = (rows + 2) * cols
    if frames.shape[0] == 4:
        early, late = active[:block], active[block:]
        left = [jnp.concatenate([jnp.zeros_like(early), early], axis=0), active]
        w_time = w_time_ref[features:, :]
    else:
        left = [active[a * block : (a + 2) * block] for a in range(3)]
        w_time = w_time_ref[...]
    left = jnp.concatenate(left, axis=1)
    halves = [jnp.dot(left, w_time[:, n : n + features], preferred_element_type=jnp.float32) for n in (0, features)]
    timed = jnp.concatenate(halves, axis=1)
    upsample(timed + b_time_ref[...][None, :], taps_ref, b_up_ref, out_ref, *scratch, rows, cols)


def prepare_taps(w_up_ref, taps_ref):
    features = w_up_ref.shape[1]
    out_width = taps_ref.shape[-1]
    for e in range(3):
        taps = [w_up_ref[(b * 3 + e) * out_width : (b * 3 + e + 1) * out_width, :].T for b in range(3)]
        top, middle, bottom = (x.astype(jnp.float32) for x in taps)
        taps_ref[0, e, :features] = taps[0]
        taps_ref[0, e, features:] = (middle + bottom).astype(taps_ref.dtype)
        taps_ref[1, e, :features] = (top + middle).astype(taps_ref.dtype)
        taps_ref[1, e, features:] = taps[2]


def upsample(timed, taps_ref, b_up_ref, out_ref, wide_ref, done_ref, sems, rows, cols):
    space, space_count = lax.axis_index("space"), lax.axis_size("space")
    features = timed.shape[1] // 2
    tall = rows + 2
    frames = timed.shape[0] // (tall * cols)
    out_width = done_ref.shape[-1]
    timed = timed.astype(jnp.bfloat16)

    def timed_row(f, h, r):
        x = timed[(f * tall + r) * cols : (f * tall + r + 1) * cols, h * features : (h + 1) * features]
        if r == 0:
            x = jnp.where(space > 0, x, jnp.zeros_like(x))
        if r == tall - 1:
            x = jnp.where(space < space_count - 1, x, jnp.zeros_like(x))
        return x

    doubled = [[timed_row(f, h, r) for r in range(tall)] for f in range(frames) for h in range(2)]
    copies = []
    for p in range(2):
        left = jnp.concatenate(
            [jnp.concatenate([frame[r + p + k] for frame in doubled for r in range(rows)], axis=0) for k in range(2)], axis=1
        )
        sums = [jnp.dot(left, taps_ref[p, e], preferred_element_type=jnp.float32) for e in range(3)]
        middle = sums[1] + b_up_ref[...][None, :]
        even = column_shift(sums[0], 1, cols) + (middle + sums[2])
        odd = column_shift(sums[2], -1, cols) + (middle + sums[0])
        half = even.shape[0]
        for q, x in enumerate((even, odd)):
            wide_ref[p, 0, pl.ds(q, half, stride=2), :] = x[:, :LANES]
            wide_ref[p, 1, pl.ds(q, half, stride=2), pl.ds(0, out_width - LANES)] = x[:, LANES:]
        low, high = wide_ref[p, 0], wide_ref[p, 1, :, pl.ds(0, out_width - LANES)]
        place = done_ref.shape[1:-1]
        done_ref[p, :, :, :, :LANES] = low.astype(done_ref.dtype).reshape(place + (LANES,))
        done_ref[p, :, :, :, LANES:] = high.astype(done_ref.dtype).reshape(place + (out_width - LANES,))
        copies.append(pltpu.make_async_copy(done_ref.at[p], out_ref.at[:, :, p], sems.at[p]))
        copies[-1].start()
    for copy in copies:
        copy.wait()


def first_kernel(
    own_ref, w_in_ref, b_in_ref, gain_ref, b_time_ref, b_up_ref, w_time_ref, w_up_ref, out_ref, taps_ref, *scratch, rows, width
):
    time = lax.axis_index("tm")

    @pl.when(time == 0)
    def _():
        prepare_taps(w_up_ref, taps_ref)
        frames = jnp.concatenate([jnp.zeros_like(own_ref), own_ref[...]], axis=0)
        finish(frames, w_in_ref, b_in_ref, gain_ref, b_time_ref, b_up_ref, w_time_ref, taps_ref, out_ref, scratch, rows, width)

    @pl.when(time > 0)
    def _():
        prepare_taps(w_up_ref, taps_ref)


def second_kernel(
    own_ref, one_ref, w_in_ref, b_in_ref, gain_ref, b_time_ref, b_up_ref, w_time_ref, taps_ref, _out,
    out_ref, *scratch, rows, width,
):
    @pl.when(lax.axis_index("tm") == 1)
    def _():
        frames = jnp.concatenate([jnp.zeros_like(one_ref), one_ref[...], own_ref[...]], axis=0)
        finish(frames, w_in_ref, b_in_ref, gain_ref, b_time_ref, b_up_ref, w_time_ref, taps_ref, out_ref, scratch, rows, width)


def third_kernel(
    own_ref, near_ref, two_ref, w_in_ref, b_in_ref, gain_ref, b_time_ref, b_up_ref, w_time_ref, taps_ref, _out,
    out_ref, *scratch, rows, width, mine,
):
    @pl.when(mine(lax.axis_index("tm")))
    def _():
        frames = jnp.concatenate([two_ref[...], near_ref[...], own_ref[...]], axis=0)
        finish(frames, w_in_ref, b_in_ref, gain_ref, b_time_ref, b_up_ref, w_time_ref, taps_ref, out_ref, scratch, rows, width)


def params(mib):
    return pltpu.CompilerParams(vmem_limit_bytes=mib * 1024 * 1024)


def shards(latent, w_in, b_in, gain_in, w_time, b_time, w_up, b_up):
    frames, rows, cols, width = latent.shape
    features = w_in.shape[-1]
    out_width = w_up.shape[-1]
    w_time = in_hbm(w_time.reshape(-1, w_time.shape[-1]))
    w_up = in_hbm(jnp.swapaxes(w_up, 2, 3).reshape(-1, w_up.shape[2]))
    out_shape = (2 * frames, rows, 2, 2 * cols, out_width)

    even = swapped(latent, "space", 0)
    odd = swapped(latent, "space", 1)
    arrays = [w_time, w_up] + [in_hbm(x) for x in (w_in.reshape(-1, features), b_in, gain_in, b_time, b_up, latent)]
    w_time, w_up, w_in, b_in, gain_in, b_time, b_up, own = pl.pallas_call(
        stage_kernel,
        out_shape=[pltpu.VMEM(x.shape, x.dtype) for x in arrays],
        in_specs=[HBM] * len(arrays),
        out_specs=[VMEM] * len(arrays),
        scratch_shapes=[pltpu.SemaphoreType.DMA((len(arrays),))],
        compiler_params=params(1),
    )(*arrays)
    own = pl.pallas_call(
        pack_kernel,
        out_shape=pltpu.VMEM((frames, cols, LANES), latent.dtype),
        in_specs=[VMEM] * 3,
        out_specs=VMEM,
        compiler_params=params(1),
    )(odd, even, own)
    times = lax.axis_size("tm")

    def in_first(t, s):
        return (t, s ^ 1) if t > 2 else (0, s ^ 1) if t == 2 else (t + 1, s)

    def by_two(t, s):
        if t + 2 < times:
            return t + 2, s
        last = t == times - 1
        return (0, s if last else s ^ 1) if s % 2 else (1, s ^ 1 if last else s)

    def in_last(t, s):
        return (t, s ^ 1) if t < 2 else (2, s) if t == times - 1 else (t + 1, s)

    first, two, one = moved(own, in_first), moved(own, by_two), moved(own, in_last)

    scratch = [
        pltpu.VMEM((2, 2, 2 * frames * rows * 2 * cols, LANES), jnp.float32),
        pltpu.VMEM((2, 2 * frames, rows, 2 * cols, out_width), jnp.bfloat16),
        pltpu.SemaphoreType.DMA((2,)),
    ]
    result = pltpu.HBM(out_shape, jnp.bfloat16)
    out, taps = pl.pallas_call(
        functools.partial(first_kernel, rows=rows, width=width),
        out_shape=[result, pltpu.VMEM((2, 3, 2 * features, out_width), jnp.bfloat16)],
        in_specs=[VMEM] * 8,
        out_specs=[HBM, VMEM],
        scratch_shapes=scratch,
        compiler_params=params(16),
    )(own, w_in, b_in, gain_in, b_time, b_up, w_time, w_up)
    out = pl.pallas_call(
        functools.partial(second_kernel, rows=rows, width=width),
        out_shape=result,
        in_specs=[VMEM] * 9 + [HBM],
        out_specs=HBM,
        scratch_shapes=scratch,
        input_output_aliases={9: 0},
        compiler_params=params(16),
    )(own, first, w_in, b_in, gain_in, b_time, b_up, w_time, taps, out)
    for near, mine in ((first, lambda time: time == 2), (one, lambda time: time > 2)):
        out = pl.pallas_call(
            functools.partial(third_kernel, rows=rows, width=width, mine=mine),
            out_shape=result,
            in_specs=[VMEM] * 10 + [HBM],
            out_specs=HBM,
            scratch_shapes=scratch,
            input_output_aliases={10: 0},
            compiler_params=params(16),
        )(own, near, two, w_in, b_in, gain_in, b_time, b_up, w_time, taps, out)
    return out.reshape(2 * frames, 2 * rows, 2 * cols, out_width)


def solution(mesh):
    in_specs = (P(("clips", "tm"), "space", None, None), P(), P(), P(), P(), P(), P(), P())
    out_specs = P(("clips", "tm"), "space", None, None)
    return jax.shard_map(shards, mesh=mesh, in_specs=in_specs, out_specs=out_specs, check_vma=False)
```
